128 devices in a mesh: row: 16 (over x, z), col: 8 (over y, core).
Axes of the slice: x: 4, y: 4, z: 4, core: 2. Of those that a mesh axis runs over, the one named last changes fastest.
Arguments:
- cam_jac: float32 [8192, 36, 128], P(('row', 'col')), may hold values from -6 to 6
- pt_jac: float32 [8192, 12, 128], P(('row', 'col')), may hold values from -6 to 6
- resid: float32 [8192, 4, 128], P(('row', 'col')), may hold values from -0.3 to 0.3
- damping: float32 [8192, 128], P(('row', 'col')), may hold values from 0.5 to 4
- cams: int32 [8192, 2, 128], P(('row', 'col')), may hold values from 0 to 127
- block_pair: int32 [8192, 1], P(('row', 'col')), may hold values from 0 to 63; in each aligned block of 64 rows (0 to 63, 64 to 127, ...) at most 2 rows name the same one
- pair_sides: int32 [64, 2], replicated, may hold values from 0 to 127, as said below
- cluster_home: int32 [32], replicated, may hold values from 0 to 31, each once
Outputs:
- schur_blocks: float32 [128, 1152, 1152], P(('row', 'col'))
- reduced_rhs: float32 [32, 1152], P('row', 'col')
The draws below stay inside these ranges and needn't reach their ends.
Inputs may be any that keep to these rules, and one draw needn't show every extreme that they name: `pair_sides`: every side 0 to 127 appears exactly once. `block_pair`: among the 64 blocks of one device no pair is named more than 2 times, a bound that some block reaches.
All inputs are finite; a program needn't handle non-finite values.
Results may differ from the reference program's by a relative error of at most 0.0003.
Values sent between devices are 32-bit elements; how exact they have to be, the bound alone decides.
No kernel may reach another device: no remote copies, remote signals or barrier semaphores. Data moves between devices by JAX's collectives and lax.ppermute only.
A program may use at most 192 MiB of HBM per device.

```python
import math
import jax
import jax.numpy as jnp
import numpy as np
from jax import lax

CAMS = 128
PTS = 128
NB_DEV = 64
NBR = 4
CLUSTERS = 32
SIDES = 128
PAIRS = 64
BLOCKS = 8192
MOST = 2


def draw_pair_sides(key, part):
    key = jax.random.fold_in(key, 11)
    order = jax.random.permutation(key, SIDES)
    return order.reshape(PAIRS, 2).astype(jnp.int32)


def touch_ends(drawn, own_key, least, largest):
    longest = drawn.shape.index(max(drawn.shape))
    spots = []
    for shift in (0, 1):
        where = [jax.random.randint(jax.random.fold_in(own_key, axis), (), 0, length) for axis, length in enumerate(drawn.shape)]
        where[longest] = (where[longest] + shift) % drawn.shape[longest]
        spots.append(tuple(where))
    return drawn.at[spots[0]].set(least).at[spots[1]].set(largest)


def block_scale(stream_key, extent, shards, least, top_value):
    def one(position, shards_of):
        steps = jax.random.uniform(jax.random.fold_in(jax.random.fold_in(stream_key, 6), position), (shards_of,), jnp.float32, least / len(shards), top_value / len(shards))
        return jnp.repeat(jnp.exp(steps), extent[position] // shards_of).reshape((-1,) + (1,) * (len(extent) - position - 1))

    loudness = one(*shards[0])
    for cut in shards[1:]:
        loudness = loudness * one(*cut)
    return loudness


def deal_out(stream_key, own, number, rows, count, top, most, slope):
    order = jax.random.permutation(stream_key, count)
    heavy_load, common = load_shares(count, rows * top, most, slope, True), load_shares(count, rows * top, most, slope, False)
    places = jnp.arange(count)

    def named(tallies, rotation):
        used = int((tallies > 0).sum())
        fixed = max(1, used // 4)
        moved = fixed + (places - fixed + rotation * (used - fixed)) % max(1, count - fixed)
        return jnp.zeros((count,), jnp.int32).at[order[jnp.where(places < fixed, places, moved)]].set(jnp.asarray(tallies, jnp.int32))

    tallies = jnp.where(number % 4 == 0, named(heavy_load, number // 4), named(common, number - number // 4 - 1))
    mixed = jax.random.permutation(jax.random.fold_in(own, 3), count)
    source_of, sink = mixed[0:count // 2 * 2:2], mixed[1:count // 2 * 2:2]
    room = jnp.minimum(tallies[source_of] - 1, most - tallies[sink]) // 2
    room = jnp.where((source_of == order[0]) | (sink == order[0]) | (tallies[sink] == 0), 0, jnp.maximum(room, 0))
    moved = jax.random.randint(jax.random.fold_in(own, 4), (count // 2,), 0, 1 << 20) % (room + 1)
    tallies = tallies.at[source_of].add(-moved).at[sink].add(moved)
    labels = jnp.searchsorted(jnp.cumsum(tallies), jnp.arange(rows * top), side="right").astype(jnp.int32)
    table = labels.reshape(top, rows).T
    table = table[jax.random.permutation(jax.random.fold_in(own, 1), rows)]
    rotation = jax.random.randint(jax.random.fold_in(own, 2), (rows, 1), 0, top)
    return jnp.take_along_axis(table, (jnp.arange(top)[None, :] + rotation) % top, axis=1)


def load_shares(number_of, total, limit, lean, full):
    weights = [(1 << 20) // math.isqrt(grade ** lean) + 1 for grade in range(1, number_of + 1)]
    largest = limit if full else min(limit, max(-(-total // number_of), total * weights[0] // sum(weights)))
    least = 1 if total - largest >= number_of - 1 else 0
    given, rest = [largest] + [least] * (number_of - 1), total - largest - least * (number_of - 1)
    while rest > 0:
        candidates = [i for i in range(1, number_of) if given[i] < largest] or [i for i in range(1, number_of) if given[i] < limit]
        mass, budget = sum([weights[i] for i in candidates]), rest
        for i in candidates:
            extra = min(limit - given[i], max(1, budget * weights[i] // mass), rest)
            given[i] = given[i] + extra
            rest = rest - extra
    return np.array(given)


def bell_draw(own_key, extent, scale, limit, shards=(), held_as=jnp.bfloat16):
    values = scale * jax.random.normal(own_key, extent, jnp.float32)
    if shards:
        values = values * block_scale(own_key, extent, shards, -0.22, 0.18)
    return jnp.clip(values, -limit, limit).astype(held_as)


def setup_inputs(seed: int = 0) -> dict:
    seeds = jax.random.split(jax.random.key(seed), 9)
    cam_jac = bell_draw(seeds[0], (BLOCKS, 36, PTS), 1.0, 6.0, ((0, 128),), jnp.float32)
    pt_jac = bell_draw(seeds[1], (BLOCKS, 12, PTS), 1.0, 6.0, ((0, 128),), jnp.float32)
    resid = bell_draw(seeds[2], (BLOCKS, 4, PTS), 0.05, 0.3, ((0, 128),), jnp.float32)
    damping = jnp.clip(jnp.exp(math.log(4.0) - 2.0794415 * jax.random.uniform(seeds[3], (BLOCKS, PTS), jnp.float32) ** block_scale(seeds[3], (BLOCKS, PTS), ((0, 128),), -0.2, 0.2)), 0.5, 4.0)
    cams = touch_ends(jax.random.randint(seeds[4], (BLOCKS, 2, PTS), 0, CAMS), jax.random.fold_in(seeds[4], 1), 0, CAMS - 1).astype(jnp.int32)
    block_pair_keys = jax.random.split(jax.random.fold_in(seeds[5], 1), BLOCKS // NB_DEV)
    block_pair_turns = jax.random.permutation(jax.random.fold_in(seeds[5], 3), BLOCKS // NB_DEV)
    block_pair = jax.vmap(lambda own, number: deal_out(jax.random.fold_in(seeds[5], 2), own, number, NB_DEV, PAIRS, 1, MOST, 2))(block_pair_keys, block_pair_turns).reshape((BLOCKS, 1))
    pair_sides = draw_pair_sides(jax.random.fold_in(seeds[8], 71), 0)
    cluster_home = jax.random.permutation(seeds[7], CLUSTERS).astype(jnp.int32)
    return dict(cam_jac=cam_jac, pt_jac=pt_jac, resid=resid, damping=damping, cams=cams, block_pair=block_pair, pair_sides=pair_sides, cluster_home=cluster_home)


def invert_three(matrix):
    cofactor_rows = []
    for row_pick in range(3):
        entries = []
        for col_pick in range(3):
            entries.append(matrix[:, (col_pick + 1) % 3, (row_pick + 1) % 3] * matrix[:, (col_pick + 2) % 3, (row_pick + 2) % 3]
                           - matrix[:, (col_pick + 1) % 3, (row_pick + 2) % 3] * matrix[:, (col_pick + 2) % 3, (row_pick + 1) % 3])
        cofactor_rows.append(jnp.stack(entries, axis=1))
    adjugate = jnp.stack(cofactor_rows, axis=1)
    determinant = matrix[:, 0, 0] * adjugate[:, 0, 0] + matrix[:, 0, 1] * adjugate[:, 1, 0] + matrix[:, 0, 2] * adjugate[:, 2, 0]
    return adjugate / determinant[:, None, None, :]


def point_terms(cam_jac, pt_jac, resid, damping):
    blocks_here = cam_jac.shape[0]
    points_here = cam_jac.shape[-1]
    camera_rows = cam_jac.reshape(blocks_here, 2, 2, 9, points_here)
    point_rows = pt_jac.reshape(blocks_here, 2, 2, 3, points_here)
    errors = resid.reshape(blocks_here, 2, 2, points_here)
    hessian = jnp.sum(point_rows[:, :, :, :, None, :] * point_rows[:, :, :, None, :, :], axis=(1, 2))
    hessian = hessian + damping[:, None, None, :] * jnp.eye(3, dtype=jnp.float32)[None, :, :, None]
    inverse = invert_three(hessian)
    coupling = jnp.sum(camera_rows[:, :, :, :, None, :] * point_rows[:, :, :, None, :, :], axis=2)
    cam_grad = jnp.sum(camera_rows * errors[:, :, :, None, :], axis=2)
    point_grad = jnp.sum(point_rows * errors[:, :, :, None, :], axis=(1, 2))
    shifted = jnp.sum(inverse * point_grad[:, None, :, :], axis=2)
    scaled = jnp.sum(coupling[:, :, :, :, None, :] * inverse[:, None, None, :, :, :], axis=3)
    reduced = cam_grad - jnp.sum(coupling * shifted[:, None, None, :, :], axis=3)
    return coupling, scaled, reduced


def reference(cam_jac, pt_jac, resid, damping, cams, block_pair, pair_sides, cluster_home):
    width = 9 * CAMS
    groups = cam_jac.shape[0] // NB_DEV
    nine = jnp.arange(9, dtype=jnp.int32)

    def split(array):
        return array.reshape((groups, NB_DEV) + array.shape[1:])

    def step(carry, inputs):
        schur_flat, rhs_flat = carry
        cam_part, point_part, error_part, damp_part, cam_ids, pair_part = inputs
        coupling, scaled, reduced = point_terms(cam_part, point_part, error_part, damp_part)
        sides = pair_sides[pair_part[:, 0]].astype(jnp.int32)
        homes = cluster_home[sides // NBR].astype(jnp.int32)
        slots = homes * NBR + sides % NBR
        rhs_index = homes[:, :, None, None] * width + cam_ids[:, :, None, :] * 9 + nine[None, None, :, None]
        rhs_flat = rhs_flat.at[rhs_index.reshape(-1)].add(reduced.reshape(-1))
        partner = coupling[:, ::-1]
        other_cams = cam_ids[:, ::-1]
        product = jnp.sum(scaled[:, :, :, None, :, :] * partner[:, :, None, :, :, :], axis=4)
        index = (slots[:, :, None, None, None] * (width * width)
                 + (cam_ids[:, :, None, None, :] * 9 + nine[None, None, :, None, None]) * width
                 + other_cams[:, :, None, None, :] * 9 + nine[None, None, None, :, None])
        schur_flat = schur_flat.at[index.reshape(-1)].add(product.reshape(-1))
        return (schur_flat, rhs_flat), None

    start = (jnp.zeros((SIDES * width * width,), jnp.float32), jnp.zeros((CLUSTERS * width,), jnp.float32))
    inputs = (split(cam_jac), split(pt_jac), split(resid), split(damping), split(cams), split(block_pair))
    (schur_flat, rhs_flat), unused = lax.scan(step, start, inputs)
    return (-schur_flat).reshape(SIDES, width, width), rhs_flat.reshape(CLUSTERS, width)
```

```python
import functools

import jax
import jax.numpy as jnp
from jax import lax
from jax.experimental import pallas as pl
from jax.experimental.pallas import tpu as pltpu
from jax.sharding import PartitionSpec as P

CAMS = 128
PTS = 128
WIDTH = 9 * CAMS
NBR = 4
SIDES = 128
CLUSTERS = 32
BLK = 40
GROUP = 8
TABLES = 4
UNROLL = 32
FINAL = 8
FEATS = 88
VMEM_LIMIT = 60 * 2**20
RC = ("row", "col")


def inverse_of(pt_ref, damp_ref):
    jp = [[[pt_ref[:, 6 * o + 3 * r + k, :] for k in range(3)] for r in range(2)] for o in range(2)]
    damp = damp_ref[...]

    def entry(a, b):
        total = jp[0][0][a] * jp[0][0][b]
        for o, r in ((0, 1), (1, 0), (1, 1)):
            total = total + jp[o][r][a] * jp[o][r][b]
        return total + damp if a == b else total

    v00, v01, v02, v11, v12, v22 = (entry(a, b) for a, b in ((0, 0), (0, 1), (0, 2), (1, 1), (1, 2), (2, 2)))
    a00 = v11 * v22 - v12 * v12
    a01 = v02 * v12 - v01 * v22
    a02 = v01 * v12 - v02 * v11
    a11 = v00 * v22 - v02 * v02
    a12 = v01 * v02 - v00 * v12
    a22 = v00 * v11 - v01 * v01
    det = v00 * a00 + v01 * a01 + v02 * a02
    inv = [[a00 / det, a01 / det, a02 / det], [a01 / det, a11 / det, a12 / det], [a02 / det, a12 / det, a22 / det]]
    return jp, inv


def slot_of(side, home_ref):
    return home_ref[side // NBR] * NBR + side % NBR


def pack_kernel(bp_ref, ps_ref, home_ref, cam_ref, pt_ref, damp_ref, cams_ref, out0_ref, out1_ref, mix_ref, seen_ref):
    blocks = cam_ref.shape[0]
    out0_ref[...] = jnp.zeros_like(out0_ref)
    out1_ref[...] = jnp.zeros_like(out1_ref)
    jp, inv = inverse_of(pt_ref, damp_ref)
    for r in range(2):
        left = [sum(jp[0][r][k] * inv[k][m] for k in range(3)) for m in range(3)]
        for q in range(2):
            mix_ref[2 * r + q] = -sum(left[m] * jp[1][q][m] for m in range(3))

    def clear(i, carry):
        seen_ref[i] = 0
        return carry

    lax.fori_loop(0, seen_ref.shape[0], clear, 0)

    def one(t, carry):
        pair = bp_ref[t, 0]
        rank = seen_ref[pair]
        seen_ref[pair] = rank + 1
        first, second = slot_of(ps_ref[pair, 0], home_ref), slot_of(ps_ref[pair, 1], home_ref)
        row0, row1 = cam_ref[t, 0:9, :], cam_ref[t, 9:18, :]
        other = [cam_ref[t, 18:27, :], cam_ref[t, 27:36, :]]
        mix = [mix_ref[k, pl.ds(t, 1), :] for k in range(4)]
        mixed = [row0 * mix[q] + row1 * mix[2 + q] for q in range(2)]
        ids = cams_ref[t].astype(jnp.float32)

        def put(out_ref, slot, a, b, ca, cb):
            out_ref[slot, 0:8, :] = a[0][0:8]
            out_ref[slot, 8:16, :] = a[1][0:8]
            out_ref[slot, 16:24, :] = b[0][0:8]
            out_ref[slot, 24:32, :] = b[1][0:8]
            out_ref[slot, 32:33, :] = a[0][8:9]
            out_ref[slot, 33:34, :] = a[1][8:9]
            out_ref[slot, 34:35, :] = b[0][8:9]
            out_ref[slot, 35:36, :] = b[1][8:9]
            out_ref[slot, 36:37, :] = ca
            out_ref[slot, 37:38, :] = cb

        def both(out_ref):
            put(out_ref, first, mixed, other, ids[0:1], ids[1:2])
            put(out_ref, second, other, mixed, ids[1:2], ids[0:1])

        @pl.when(rank == 0)
        def _():
            both(out0_ref)

        @pl.when(rank != 0)
        def _():
            both(out1_ref)

        return carry

    lax.fori_loop(0, blocks, one, 0)


def rhs_kernel(bp_ref, ps_ref, home_ref, cam_ref, pt_ref, res_ref, damp_ref, cams_ref, out_ref, w_ref):
    blocks = cam_ref.shape[0]
    out_ref[...] = jnp.zeros_like(out_ref)
    jp, inv = inverse_of(pt_ref, damp_ref)
    err = [[res_ref[:, 2 * o + r, :] for r in range(2)] for o in range(2)]
    gp = [sum(jp[o][r][k] * err[o][r] for o in range(2) for r in range(2)) for k in range(3)]
    z = [sum(inv[k][m] * gp[m] for m in range(3)) for k in range(3)]
    for o in range(2):
        for r in range(2):
            w_ref[2 * o + r] = err[o][r] - sum(jp[o][r][k] * z[k] for k in range(3))
    number = lax.broadcasted_iota(jnp.int32, (CAMS, PTS), 0)

    def one(t, carry):
        pair = bp_ref[t, 0]
        for o in range(2):
            home = home_ref[ps_ref[pair, o] // NBR]
            b = cam_ref[t, 18 * o : 18 * o + 9, :] * w_ref[2 * o, pl.ds(t, 1), :]
            b = b + cam_ref[t, 18 * o + 9 : 18 * o + 18, :] * w_ref[2 * o + 1, pl.ds(t, 1), :]
            b = jnp.concatenate([b, jnp.zeros((7, PTS), jnp.float32)], axis=0)
            high = b.astype(jnp.bfloat16)
            low = (b - high.astype(jnp.float32)).astype(jnp.bfloat16)
            hit = jnp.where(number == cams_ref[t, o : o + 1, :], 1.0, 0.0).astype(jnp.bfloat16)
            added = lax.dot_general(
                jnp.concatenate([high, low], axis=0), hit, (((1,), (1,)), ((), ())), preferred_element_type=jnp.float32
            )
            out_ref[home] = out_ref[home] + (added[0:16] + added[16:32])
        return carry

    lax.fori_loop(0, blocks, one, 0)


def expand(block):
    a0, a1, b0, b1 = block[0:8], block[8:16], block[16:24], block[24:32]
    a08, a18, b08, b18 = block[32:33], block[33:34], block[34:35], block[35:36]
    rows = [a0 * b0[j : j + 1] + a1 * b1[j : j + 1] for j in range(8)]
    rows.append(a0 * b08 + a1 * b18)
    rows.append(a08 * b0 + a18 * b1)
    rows.append(jnp.broadcast_to(a08 * b08 + a18 * b18, (8, PTS)))
    return rows


def accumulate(idx_ref, in_ref, pay_ref, tabs):
    for g in range(GROUP):
        rows = expand(in_ref[g])
        rows.append(jnp.zeros((CAMS - FEATS, PTS), jnp.float32))
        pay_ref[pl.ds(g * PTS, PTS), :] = jnp.concatenate(rows, axis=0).T

    def body(q, carry):
        base = pl.multiple_of(q * UNROLL, UNROLL)
        for u in range(UNROLL):
            i = idx_ref[0, 0, base + u]
            tab = tabs[u % TABLES]
            tab[pl.ds(i, 1), :] = tab[pl.ds(i, 1), :] + pay_ref[pl.ds(base + u, 1), :]
        return carry

    lax.fori_loop(0, GROUP * PTS // UNROLL, body, 0)


def first_kernel(steps, idx_ref, in_ref, out_ref, pay_ref, *tabs):
    step = pl.program_id(0)
    part = out_ref.shape[0]

    @pl.when(step == 0)
    def _():
        for tab in tabs:
            tab[...] = jnp.zeros_like(tab)

    @pl.when(step < steps)
    def _():
        accumulate(idx_ref, in_ref, pay_ref, tabs)

    @pl.when(step >= steps)
    def _():
        rows = pl.ds(pl.multiple_of((step - steps) * part, part), part)
        total = tabs[0][rows, :]
        for tab in tabs[1:]:
            total = total + tab[rows, :]
        out_ref[...] = total


def last_kernel(steps, idx_ref, in_ref, start_ref, out_ref, pay_ref, spread_ref, wide_ref, *tabs):
    step = pl.program_id(0)

    @pl.when(step == 0)
    def _():
        for tab in tabs:
            tab[...] = jnp.zeros_like(tab)
        source = lax.broadcasted_iota(jnp.int32, (CAMS, WIDTH), 0) * 9
        lane = lax.broadcasted_iota(jnp.int32, (CAMS, WIDTH), 1)
        spread = jnp.where((lane >= source) & (lane < source + 9), 1.0, 0.0).astype(jnp.bfloat16)
        spread_ref[0:CAMS, :] = spread
        spread_ref[CAMS : 2 * CAMS, :] = spread

    @pl.when(step < steps)
    def _():
        accumulate(idx_ref, in_ref, pay_ref, tabs)

    @pl.when(step >= steps)
    def _():
        base = pl.multiple_of((step - steps) * FINAL * CAMS, FINAL * CAMS)
        parts = []
        for c in range(FINAL):
            rows = pl.ds(base + c * CAMS, CAMS)
            total = start_ref[rows, :]
            for tab in tabs:
                total = total + tab[rows, :]
            total = total.T[0:FEATS]
            high = total.astype(jnp.bfloat16)
            low = (total - high.astype(jnp.float32)).astype(jnp.bfloat16)
            parts.append(jnp.concatenate([high, low], axis=1))
        wide_ref[...] = jnp.dot(jnp.concatenate(parts, axis=0), spread_ref[...], preferred_element_type=jnp.float32)
        lane = lax.broadcasted_iota(jnp.int32, (8, WIDTH), 1)
        which = lane % 9
        sub = lax.broadcasted_iota(jnp.int32, (8, WIDTH), 0)
        for c in range(FINAL):
            at = c * FEATS
            eight = wide_ref[at : at + 8, :]
            for j in range(1, 9):
                eight = jnp.where(which == j, wide_ref[at + 8 * j : at + 8 * j + 8, :], eight)
            last = jnp.sum(jnp.where(which == sub, wide_ref[at + 72 : at + 80, :], 0.0), axis=0, keepdims=True)
            last = jnp.where(which[0:1] == 8, wide_ref[at + 80 : at + 81, :], last)
            out_ref[0, 9 * c : 9 * c + 8, :] = eight
            out_ref[0, 9 * c + 8 : 9 * c + 9, :] = last


def params(**more):
    return pltpu.CompilerParams(vmem_limit_bytes=VMEM_LIMIT, **more)


def index_of(arrived):
    cell = arrived[:, 36, :] * CAMS + arrived[:, 37, :]
    return cell.astype(jnp.int32).reshape(SIDES // GROUP, 1, GROUP * PTS)


def local(cam_jac, pt_jac, resid, damping, cams, block_pair, pair_sides, cluster_home):
    smem = pl.BlockSpec(memory_space=pltpu.SMEM)
    vmem = pl.BlockSpec(memory_space=pltpu.VMEM)
    blocks = cam_jac.shape[0]
    sent = jax.ShapeDtypeStruct((SIDES, BLK, PTS), jnp.float32)
    out0, out1 = pl.pallas_call(
        pack_kernel,
        in_specs=[smem] * 3 + [vmem] * 4,
        out_specs=[vmem, vmem],
        out_shape=[sent, sent],
        scratch_shapes=[pltpu.VMEM((4, blocks, PTS), jnp.float32), pltpu.SMEM((pair_sides.shape[0],), jnp.int32)],
        compiler_params=params(),
        name="pack",
    )(block_pair, pair_sides, cluster_home, cam_jac, pt_jac, damping, cams)
    in0 = lax.all_to_all(out0, RC, 0, 0, tiled=True)
    in1 = lax.all_to_all(out1, RC, 0, 0, tiled=True)

    partial = pl.pallas_call(
        rhs_kernel,
        in_specs=[smem] * 3 + [vmem] * 5,
        out_specs=vmem,
        out_shape=jax.ShapeDtypeStruct((CLUSTERS, 16, CAMS), jnp.float32),
        scratch_shapes=[pltpu.VMEM((4, blocks, PTS), jnp.float32)],
        compiler_params=params(),
        cost_estimate=pl.CostEstimate(flops=10**8, bytes_accessed=3 * 10**6, transcendentals=0),
        name="rhs",
    )(block_pair, pair_sides, cluster_home, cam_jac, pt_jac, resid, damping, cams)
    rows, cols = lax.axis_size("row"), lax.axis_size("col")
    shares = partial[:, 0:9].reshape(rows, CLUSTERS // rows, 9, cols, CAMS // cols)
    shares = jnp.transpose(shares, (0, 3, 1, 2, 4)).reshape(rows * cols, -1)
    share = lax.psum_scatter(shares, RC, scatter_dimension=0, tiled=True)
    share = share.reshape(CLUSTERS // rows, 9, CAMS // cols)
    reduced_rhs = jnp.transpose(share, (0, 2, 1)).reshape(CLUSTERS // rows, WIDTH // cols)

    steps = SIDES // GROUP
    cells = CAMS * CAMS
    part = 2048
    spec_idx = pl.BlockSpec((1, 1, GROUP * PTS), lambda s: (jnp.minimum(s, steps - 1), 0, 0), memory_space=pltpu.SMEM)
    spec_in = pl.BlockSpec((GROUP, BLK, PTS), lambda s: (jnp.minimum(s, steps - 1), 0, 0))
    tabs = [pltpu.VMEM((cells, PTS), jnp.float32)] * TABLES
    pay = pltpu.VMEM((GROUP * PTS, PTS), jnp.float32)
    cost = pl.CostEstimate(flops=6 * 10**9, bytes_accessed=12 * 10**6, transcendentals=0)
    total = pl.pallas_call(
        functools.partial(first_kernel, steps),
        grid=(steps + cells // part,),
        in_specs=[spec_idx, spec_in],
        out_specs=pl.BlockSpec((part, PTS), lambda s: (jnp.maximum(s - steps, 0), 0)),
        out_shape=jax.ShapeDtypeStruct((cells, PTS), jnp.float32),
        scratch_shapes=[pay] + tabs,
        compiler_params=params(),
        cost_estimate=cost,
        name="first",
    )(index_of(in0), in0)
    schur = pl.pallas_call(
        functools.partial(last_kernel, steps),
        grid=(steps + CAMS // FINAL,),
        in_specs=[spec_idx, spec_in, vmem],
        out_specs=pl.BlockSpec((1, 9 * FINAL, WIDTH), lambda s: (0, jnp.maximum(s - steps, 0), 0)),
        out_shape=jax.ShapeDtypeStruct((1, WIDTH, WIDTH), jnp.float32),
        scratch_shapes=[
            pay,
            pltpu.VMEM((2 * CAMS, WIDTH), jnp.bfloat16),
            pltpu.VMEM((FINAL * FEATS, WIDTH), jnp.float32),
        ]
        + tabs,
        compiler_params=params(),
        cost_estimate=cost,
        name="last",
    )(index_of(in1), in1, total)
    return schur, reduced_rhs


def solution(mesh):
    return jax.shard_map(
        local,
        mesh=mesh,
        in_specs=(
            P(RC, None, None),
            P(RC, None, None),
            P(RC, None, None),
            P(RC, None),
            P(RC, None, None),
            P(RC, None),
            P(),
            P(),
        ),
        out_specs=(P(RC, None, None), P("row", "col")),
        check_vma=False,
    )
```

```python
import functools

import jax
import jax.numpy as jnp
from jax import lax
from jax.experimental import pallas as pl
from jax.experimental.pallas import tpu as pltpu
from jax.sharding import PartitionSpec as P

CAMS = 128
PTS = 128
WIDTH = 9 * CAMS
NBR = 4
SIDES = 128
CLUSTERS = 32
BLK = 40
GROUP = 8
TABLES = 4
UNROLL = 32
FINAL = 8
FEATS = 88
VMEM_LIMIT = 60 * 2**20
RC = ("row", "col")


def inverse_of(pt_ref, damp_ref):
    jp = [[[pt_ref[6 * o + 3 * r + k] for k in range(3)] for r in range(2)] for o in range(2)]
    damp = damp_ref[...]

    def entry(a, b):
        total = jp[0][0][a] * jp[0][0][b]
        for o, r in ((0, 1), (1, 0), (1, 1)):
            total = total + jp[o][r][a] * jp[o][r][b]
        return total + damp if a == b else total

    v00, v01, v02, v11, v12, v22 = (entry(a, b) for a, b in ((0, 0), (0, 1), (0, 2), (1, 1), (1, 2), (2, 2)))
    a00 = v11 * v22 - v12 * v12
    a01 = v02 * v12 - v01 * v22
    a02 = v01 * v12 - v02 * v11
    a11 = v00 * v22 - v02 * v02
    a12 = v01 * v02 - v00 * v12
    a22 = v00 * v11 - v01 * v01
    det = v00 * a00 + v01 * a01 + v02 * a02
    inv = [[a00 / det, a01 / det, a02 / det], [a01 / det, a11 / det, a12 / det], [a02 / det, a12 / det, a22 / det]]
    return jp, inv


def slot_of(side, home_ref):
    return home_ref[side // NBR] * NBR + side % NBR


def pack_kernel(which, *refs):
    bp_ref, ps_ref, home_ref, cam_ref, pt_ref, damp_ref, cams_ref = refs[:7]
    share_ref = refs[7] if which else None
    out_ref, rows_ref, turned_ref, seen_ref = refs[-4:]
    blocks = damp_ref.shape[0]
    out_ref[...] = jnp.zeros_like(out_ref)
    if which:
        out_ref[:, 38:40, :] = share_ref[...]
    jp, inv = inverse_of(pt_ref, damp_ref)
    mix = []
    for r in range(2):
        left = [sum(jp[0][r][k] * inv[k][m] for k in range(3)) for m in range(3)]
        mix.append([-sum(left[m] * jp[1][q][m] for m in range(3)) for q in range(2)])

    def put(row, value):
        rows_ref[pl.ds(row, blocks, stride=BLK), :] = value

    def turn(row, value):
        turned_ref[pl.ds(row, blocks, stride=8), :] = value

    for i in range(9):
        row0, row1 = cam_ref[i], cam_ref[9 + i]
        for q in range(2):
            mixed = row0 * mix[0][q] + row1 * mix[1][q]
            other = cam_ref[18 + 9 * q + i]
            if i < 8:
                put(8 * q + i, mixed)
                put(16 + 8 * q + i, other)
            else:
                put(32 + q, mixed)
                put(34 + q, other)
                turn(2 + q, mixed)
                turn(q, other)
    zero = jnp.zeros((blocks, PTS), jnp.float32)
    for o in range(2):
        ids = cams_ref[:, o, :].astype(jnp.float32)
        put(36 + o, ids)
        turn(5 - o, ids)
        put(38 + o, zero)
        turn(6 + o, zero)
    tops = 38 if which else BLK

    def clear(i, carry):
        seen_ref[i] = 0
        return carry

    lax.fori_loop(0, seen_ref.shape[0], clear, 0)

    def one(t, carry):
        pair = bp_ref[t]
        rank = seen_ref[pair]
        seen_ref[pair] = rank + 1

        @pl.when(rank == which)
        def _():
            first, second = slot_of(ps_ref[0, pair], home_ref), slot_of(ps_ref[1, pair], home_ref)
            base = pl.multiple_of(t * BLK, 8)
            out_ref[first, 0:tops, :] = rows_ref[pl.ds(base, tops), :]
            out_ref[second, 0:16, :] = rows_ref[pl.ds(base + 16, 16), :]
            out_ref[second, 16:32, :] = rows_ref[pl.ds(base, 16), :]
            out_ref[second, 32:tops, :] = turned_ref[pl.ds(pl.multiple_of(t * 8, 8), tops - 32), :]

        return carry

    lax.fori_loop(0, blocks, one, 0)


def rhs_kernel(bp_ref, ps_ref, home_ref, cam_ref, pt_ref, res_ref, damp_ref, cams_ref, out_ref, b_ref):
    blocks = damp_ref.shape[0]
    out_ref[...] = jnp.zeros_like(out_ref)
    b_ref[...] = jnp.zeros_like(b_ref)
    jp, inv = inverse_of(pt_ref, damp_ref)
    err = [[res_ref[:, 2 * o + r, :] for r in range(2)] for o in range(2)]
    gp = [sum(jp[o][r][k] * err[o][r] for o in range(2) for r in range(2)) for k in range(3)]
    z = [sum(inv[k][m] * gp[m] for m in range(3)) for k in range(3)]
    for o in range(2):
        w = [err[o][r] - sum(jp[o][r][k] * z[k] for k in range(3)) for r in range(2)]
        for i in range(9):
            value = cam_ref[18 * o + i] * w[0] + cam_ref[18 * o + 9 + i] * w[1]
            b_ref[pl.ds(16 * o + i, blocks, stride=32), :] = value
    number = lax.broadcasted_iota(jnp.int32, (CAMS, PTS), 0)

    def one(t, carry):
        pair = bp_ref[t]
        for o in range(2):
            home = home_ref[ps_ref[o, pair] // NBR]
            b = b_ref[pl.ds(pl.multiple_of(t * 32, 32) + 16 * o, 16), :]
            high = b.astype(jnp.bfloat16)
            low = (b - high.astype(jnp.float32)).astype(jnp.bfloat16)
            hit = jnp.where(number == cams_ref[t, o : o + 1, :], 1.0, 0.0).astype(jnp.bfloat16)
            added = lax.dot_general(
                jnp.concatenate([high, low], axis=0), hit, (((1,), (1,)), ((), ())), preferred_element_type=jnp.float32
            )
            out_ref[home] = out_ref[home] + (added[0:16] + added[16:32])
        return carry

    lax.fori_loop(0, blocks, one, 0, unroll=4)


def expand(block):
    a0, a1, b0, b1 = block[0:8], block[8:16], block[16:24], block[24:32]
    a08, a18, b08, b18 = block[32:33], block[33:34], block[34:35], block[35:36]
    rows = [a0 * b0[j : j + 1] + a1 * b1[j : j + 1] for j in range(8)]
    rows.append(a0 * b08 + a1 * b18)
    rows.append(a08 * b0 + a18 * b1)
    rows.append(jnp.broadcast_to(a08 * b08 + a18 * b18, (8, PTS)))
    return rows


def accumulate(idx_ref, in_ref, pay_ref, tabs):
    for g in range(GROUP):
        rows = expand(in_ref[g])
        rows.append(jnp.zeros((CAMS - FEATS, PTS), jnp.float32))
        pay_ref[pl.ds(g * PTS, PTS), :] = jnp.concatenate(rows, axis=0).T

    def body(q, carry):
        base = pl.multiple_of(q * UNROLL, UNROLL)
        for u in range(UNROLL):
            i = idx_ref[0, 0, base + u]
            tab = tabs[u % TABLES]
            tab[pl.ds(i, 1), :] = tab[pl.ds(i, 1), :] + pay_ref[pl.ds(base + u, 1), :]
        return carry

    lax.fori_loop(0, GROUP * PTS // UNROLL, body, 0)


def first_kernel(steps, idx_ref, in_ref, out_ref, pay_ref, *tabs):
    step = pl.program_id(0)
    part = out_ref.shape[0]

    @pl.when(step == 0)
    def _():
        for tab in tabs:
            tab[...] = jnp.zeros_like(tab)

    @pl.when(step < steps)
    def _():
        accumulate(idx_ref, in_ref, pay_ref, tabs)

    @pl.when(step >= steps)
    def _():
        rows = pl.ds(pl.multiple_of((step - steps) * part, part), part)
        total = tabs[0][rows, :]
        for tab in tabs[1:]:
            total = total + tab[rows, :]
        out_ref[...] = total


def last_kernel(steps, idx_ref, in_ref, start_ref, out_ref, pay_ref, spread_ref, wide_ref, *tabs):
    step = pl.program_id(0)

    @pl.when(step == 0)
    def _():
        for tab in tabs:
            tab[...] = jnp.zeros_like(tab)
        source = lax.broadcasted_iota(jnp.int32, (CAMS, WIDTH), 0) * 9
        lane = lax.broadcasted_iota(jnp.int32, (CAMS, WIDTH), 1)
        spread = jnp.where((lane >= source) & (lane < source + 9), 1.0, 0.0).astype(jnp.bfloat16)
        spread_ref[0:CAMS, :] = spread
        spread_ref[CAMS : 2 * CAMS, :] = spread

    @pl.when(step < steps)
    def _():
        accumulate(idx_ref, in_ref, pay_ref, tabs)

    @pl.when(step >= steps)
    def _():
        base = pl.multiple_of((step - steps) * FINAL * CAMS, FINAL * CAMS)
        parts = []
        for c in range(FINAL):
            rows = pl.ds(base + c * CAMS, CAMS)
            total = start_ref[rows, :]
            for tab in tabs:
                total = total + tab[rows, :]
            total = total.T[0:FEATS]
            high = total.astype(jnp.bfloat16)
            low = (total - high.astype(jnp.float32)).astype(jnp.bfloat16)
            parts.append(jnp.concatenate([high, low], axis=1))
        wide_ref[...] = jnp.dot(jnp.concatenate(parts, axis=0), spread_ref[...], preferred_element_type=jnp.float32)
        lane = lax.broadcasted_iota(jnp.int32, (8, WIDTH), 1)
        which = lane % 9
        sub = lax.broadcasted_iota(jnp.int32, (8, WIDTH), 0)
        for c in range(FINAL):
            at = c * FEATS
            eight = wide_ref[at : at + 8, :]
            for j in range(1, 9):
                eight = jnp.where(which == j, wide_ref[at + 8 * j : at + 8 * j + 8, :], eight)
            last = jnp.sum(jnp.where(which == sub, wide_ref[at + 72 : at + 80, :], 0.0), axis=0, keepdims=True)
            last = jnp.where(which[0:1] == 8, wide_ref[at + 80 : at + 81, :], last)
            out_ref[0, 9 * c : 9 * c + 8, :] = eight
            out_ref[0, 9 * c + 8 : 9 * c + 9, :] = last


def params(**more):
    return pltpu.CompilerParams(vmem_limit_bytes=VMEM_LIMIT, **more)


def index_of(arrived):
    cell = arrived[:, 36, :] * CAMS + arrived[:, 37, :]
    return cell.astype(jnp.int32).reshape(SIDES // GROUP, 1, GROUP * PTS)


def local(cam_jac, pt_jac, resid, damping, cams, block_pair, pair_sides, cluster_home):
    smem = pl.BlockSpec(memory_space=pltpu.SMEM)
    vmem = pl.BlockSpec(memory_space=pltpu.VMEM)
    blocks = cam_jac.shape[0]
    rows, cols = lax.axis_size("row"), lax.axis_size("col")
    tables = (block_pair.reshape(-1), pair_sides.T, cluster_home)
    cam_rows, pt_rows = jnp.transpose(cam_jac, (1, 0, 2)), jnp.transpose(pt_jac, (1, 0, 2))

    def pack(which, *shares):
        return pl.pallas_call(
            functools.partial(pack_kernel, which),
            in_specs=[smem] * 3 + [vmem] * (4 + len(shares)),
            out_specs=vmem,
            out_shape=jax.ShapeDtypeStruct((SIDES, BLK, PTS), jnp.float32),
            scratch_shapes=[
                pltpu.VMEM((blocks * BLK, PTS), jnp.float32),
                pltpu.VMEM((blocks * 8, PTS), jnp.float32),
                pltpu.SMEM((pair_sides.shape[0],), jnp.int32),
            ],
            compiler_params=params(),
            cost_estimate=pl.CostEstimate(flops=10**7, bytes_accessed=6 * 10**6, transcendentals=0),
            name="pack" + str(which),
        )(*tables, cam_rows, pt_rows, damping, cams, *shares)

    in0 = lax.all_to_all(pack(0), RC, 0, 0, tiled=True)

    partial = pl.pallas_call(
        rhs_kernel,
        in_specs=[smem] * 3 + [vmem] * 5,
        out_specs=vmem,
        out_shape=jax.ShapeDtypeStruct((CLUSTERS, 16, CAMS), jnp.float32),
        scratch_shapes=[pltpu.VMEM((blocks * 32, PTS), jnp.float32)],
        compiler_params=params(),
        cost_estimate=pl.CostEstimate(flops=10**10, bytes_accessed=3 * 10**6, transcendentals=0),
        name="rhs",
    )(*tables, cam_rows, pt_rows, resid, damping, cams)
    halves = partial.reshape(rows, CLUSTERS // rows, 16, CAMS)
    core = lax.axis_index("col") % 2
    mine = lax.dynamic_index_in_dim(halves, core, 1, keepdims=False)
    other = lax.dynamic_index_in_dim(halves, 1 - core, 1, keepdims=False)
    mine = mine + lax.ppermute(other, "col", [(c, c ^ 1) for c in range(cols)])
    shares = jnp.transpose(mine.reshape(rows, 16, cols, CAMS // cols), (0, 2, 1, 3))
    in1 = lax.all_to_all(pack(1, shares.reshape(SIDES, 2, PTS)), RC, 0, 0, tiled=True)
    share = jnp.sum(in1[:, 38:40, :].reshape(SIDES // 2, 2, 2, PTS), axis=0).reshape(2, 16, CAMS // cols)
    reduced_rhs = jnp.transpose(share[:, 0:9], (0, 2, 1)).reshape(2, WIDTH // cols)

    steps = SIDES // GROUP
    cells = CAMS * CAMS
    part = 2048
    spec_idx = pl.BlockSpec((1, 1, GROUP * PTS), lambda s: (jnp.minimum(s, steps - 1), 0, 0), memory_space=pltpu.SMEM)
    spec_in = pl.BlockSpec((GROUP, BLK, PTS), lambda s: (jnp.minimum(s, steps - 1), 0, 0))
    tabs = [pltpu.VMEM((cells, PTS), jnp.float32)] * TABLES
    pay = pltpu.VMEM((GROUP * PTS, PTS), jnp.float32)
    cost = pl.CostEstimate(flops=6 * 10**9, bytes_accessed=12 * 10**6, transcendentals=0)
    total = pl.pallas_call(
        functools.partial(first_kernel, steps),
        grid=(steps + cells // part,),
        in_specs=[spec_idx, spec_in],
        out_specs=pl.BlockSpec((part, PTS), lambda s: (jnp.maximum(s - steps, 0), 0)),
        out_shape=jax.ShapeDtypeStruct((cells, PTS), jnp.float32),
        scratch_shapes=[pay] + tabs,
        compiler_params=params(),
        cost_estimate=cost,
        name="first",
    )(index_of(in0), in0)
    schur = pl.pallas_call(
        functools.partial(last_kernel, steps),
        grid=(steps + CAMS // FINAL,),
        in_specs=[spec_idx, spec_in, vmem],
        out_specs=pl.BlockSpec((1, 9 * FINAL, WIDTH), lambda s: (0, jnp.maximum(s - steps, 0), 0)),
        out_shape=jax.ShapeDtypeStruct((1, WIDTH, WIDTH), jnp.float32),
        scratch_shapes=[
            pay,
            pltpu.VMEM((2 * CAMS, WIDTH), jnp.bfloat16),
            pltpu.VMEM((FINAL * FEATS, WIDTH), jnp.float32),
        ]
        + tabs,
        compiler_params=params(),
        cost_estimate=cost,
        name="last",
    )(index_of(in1), in1, total)
    return schur, reduced_rhs


def solution(mesh):
    return jax.shard_map(
        local,
        mesh=mesh,
        in_specs=(
            P(RC, None, None),
            P(RC, None, None),
            P(RC, None, None),
            P(RC, None),
            P(RC, None, None),
            P(RC, None),
            P(),
            P(),
        ),
        out_specs=(P(RC, None, None), P("row", "col")),
        check_vma=False,
    )
```

```python
import functools

import jax
import jax.numpy as jnp
from jax import lax
from jax.experimental import pallas as pl
from jax.experimental.pallas import tpu as pltpu
from jax.sharding import PartitionSpec as P

CAMS = 128
PTS = 128
WIDTH = 9 * CAMS
NBR = 4
SIDES = 128
CLUSTERS = 32
BLK = 40
GROUP = 16
TABLES = 4
FINAL = 16
FEATS = 88
VMEM_LIMIT = 60 * 2**20
RC = ("row", "col")


def inverse_of(pt_ref, damp_ref):
    jp = [[[pt_ref[6 * o + 3 * r + k] for k in range(3)] for r in range(2)] for o in range(2)]
    damp = damp_ref[...]

    def entry(a, b):
        total = jp[0][0][a] * jp[0][0][b]
        for o, r in ((0, 1), (1, 0), (1, 1)):
            total = total + jp[o][r][a] * jp[o][r][b]
        return total + damp if a == b else total

    v00, v01, v02, v11, v12, v22 = (entry(a, b) for a, b in ((0, 0), (0, 1), (0, 2), (1, 1), (1, 2), (2, 2)))
    a00 = v11 * v22 - v12 * v12
    a01 = v02 * v12 - v01 * v22
    a02 = v01 * v12 - v02 * v11
    a11 = v00 * v22 - v02 * v02
    a12 = v01 * v02 - v00 * v12
    a22 = v00 * v11 - v01 * v01
    det = v00 * a00 + v01 * a01 + v02 * a02
    inv = [[a00 / det, a01 / det, a02 / det], [a01 / det, a11 / det, a12 / det], [a02 / det, a12 / det, a22 / det]]
    return jp, inv


def slot_of(side, home_ref):
    return home_ref[side // NBR] * NBR + side % NBR


def pack_kernel(which, *refs):
    bp_ref, ps_ref, home_ref, cam_ref, pt_ref, damp_ref, cams_ref = refs[:7]
    share_ref = refs[7] if which else None
    out_ref, rows_ref, turned_ref, seen_ref = refs[-4:]
    blocks = damp_ref.shape[0]
    out_ref[:, 0:36, :] = jnp.zeros((SIDES, 36, PTS), jnp.float32)
    spots = lax.broadcasted_iota(jnp.int32, (SIDES, 4, PTS), 2)
    spots = jnp.where(lax.broadcasted_iota(jnp.int32, (SIDES, 4, PTS), 1) < 2, spots, 0)
    out_ref[:, 36:40, :] = spots.astype(jnp.float32)
    if which:
        out_ref[:, 38:40, :] = share_ref[...]
    jp, inv = inverse_of(pt_ref, damp_ref)
    mix = []
    for r in range(2):
        left = [sum(jp[0][r][k] * inv[k][m] for k in range(3)) for m in range(3)]
        mix.append([-sum(left[m] * jp[1][q][m] for m in range(3)) for q in range(2)])

    def put(row, value):
        rows_ref[pl.ds(row, blocks, stride=BLK), :] = value

    def turn(row, value):
        turned_ref[pl.ds(row, blocks, stride=8), :] = value

    for i in range(9):
        row0, row1 = cam_ref[i], cam_ref[9 + i]
        for q in range(2):
            mixed = row0 * mix[0][q] + row1 * mix[1][q]
            other = cam_ref[18 + 9 * q + i]
            if i < 8:
                put(8 * q + i, mixed)
                put(16 + 8 * q + i, other)
            else:
                put(32 + q, mixed)
                put(34 + q, other)
                turn(2 + q, mixed)
                turn(q, other)
    zero = jnp.zeros((blocks, PTS), jnp.float32)
    for o in range(2):
        ids = cams_ref[:, o, :].astype(jnp.float32)
        put(36 + o, ids)
        turn(5 - o, ids)
        put(38 + o, zero)
        turn(6 + o, zero)
    tops = 38 if which else BLK

    def clear(i, carry):
        seen_ref[i] = 0
        return carry

    lax.fori_loop(0, seen_ref.shape[0], clear, 0)

    def one(t, carry):
        pair = bp_ref[t]
        rank = seen_ref[pair]
        seen_ref[pair] = rank + 1

        @pl.when(rank == which)
        def _():
            first, second = slot_of(ps_ref[0, pair], home_ref), slot_of(ps_ref[1, pair], home_ref)
            base = pl.multiple_of(t * BLK, 8)
            out_ref[first, 0:tops, :] = rows_ref[pl.ds(base, tops), :]
            out_ref[second, 0:16, :] = rows_ref[pl.ds(base + 16, 16), :]
            out_ref[second, 16:32, :] = rows_ref[pl.ds(base, 16), :]
            out_ref[second, 32:tops, :] = turned_ref[pl.ds(pl.multiple_of(t * 8, 8), tops - 32), :]

        return carry

    lax.fori_loop(0, blocks, one, 0)


def rhs_kernel(bp_ref, ps_ref, home_ref, cam_ref, pt_ref, res_ref, damp_ref, cams_ref, out_ref, b_ref):
    blocks = damp_ref.shape[0]
    out_ref[...] = jnp.zeros_like(out_ref)
    b_ref[...] = jnp.zeros_like(b_ref)
    jp, inv = inverse_of(pt_ref, damp_ref)
    err = [[res_ref[:, 2 * o + r, :] for r in range(2)] for o in range(2)]
    gp = [sum(jp[o][r][k] * err[o][r] for o in range(2) for r in range(2)) for k in range(3)]
    z = [sum(inv[k][m] * gp[m] for m in range(3)) for k in range(3)]
    for o in range(2):
        w = [err[o][r] - sum(jp[o][r][k] * z[k] for k in range(3)) for r in range(2)]
        for i in range(9):
            value = cam_ref[18 * o + i] * w[0] + cam_ref[18 * o + 9 + i] * w[1]
            b_ref[pl.ds(16 * o + i, blocks, stride=32), :] = value
    number = lax.broadcasted_iota(jnp.int32, (CAMS, PTS), 0)

    def one(t, carry):
        pair = bp_ref[t]
        for o in range(2):
            home = home_ref[ps_ref[o, pair] // NBR]
            b = b_ref[pl.ds(pl.multiple_of(t * 32, 32) + 16 * o, 16), :]
            high = b.astype(jnp.bfloat16)
            low = (b - high.astype(jnp.float32)).astype(jnp.bfloat16)
            hit = jnp.where(number == cams_ref[t, o : o + 1, :], 1.0, 0.0).astype(jnp.bfloat16)
            added = lax.dot_general(
                jnp.concatenate([high, low], axis=0), hit, (((1,), (1,)), ((), ())), preferred_element_type=jnp.float32
            )
            out_ref[home] = out_ref[home] + (added[0:16] + added[16:32])
        return carry

    lax.fori_loop(0, blocks, one, 0, unroll=4)


def expand(block):
    a0, a1, b0, b1 = block[0:8], block[8:16], block[16:24], block[24:32]
    a08, a18, b08, b18 = block[32:33], block[33:34], block[34:35], block[35:36]
    rows = [a0 * b0[j : j + 1] + a1 * b1[j : j + 1] for j in range(8)]
    rows.append(a0 * b08 + a1 * b18)
    rows.append(a08 * b0 + a18 * b1)
    rows.append(jnp.broadcast_to(a08 * b08 + a18 * b18, (8, PTS)))
    return rows


def accumulate(idx_ref, in_ref, pay_ref, tabs):
    def widen(g):
        rows = expand(in_ref[g])
        rows.append(jnp.zeros((CAMS - FEATS, PTS), jnp.float32))
        pay_ref[g * PTS : (g + 1) * PTS, :] = jnp.concatenate(rows, axis=0).T

    widen(0)
    for g in range(GROUP):
        if g + 1 < GROUP:
            widen(g + 1)
        for u in range(g * PTS, (g + 1) * PTS):
            i = idx_ref[0, 0, u]
            tab = tabs[u % TABLES]
            tab[pl.ds(i, 1), :] = tab[pl.ds(i, 1), :] + pay_ref[u : u + 1, :]


def first_kernel(steps, idx_ref, in_ref, out_ref, pay_ref, *tabs):
    step = pl.program_id(0)
    part = out_ref.shape[0]

    @pl.when(step == 0)
    def _():
        for tab in tabs:
            tab[...] = jnp.zeros_like(tab)

    @pl.when(step < steps)
    def _():
        accumulate(idx_ref, in_ref, pay_ref, tabs)

    @pl.when(step >= steps)
    def _():
        rows = pl.ds(pl.multiple_of((step - steps) * part, part), part)
        total = tabs[0][rows, :]
        for tab in tabs[1:]:
            total = total + tab[rows, :]
        out_ref[...] = total


def last_kernel(steps, idx_ref, in_ref, start_ref, out_ref, pay_ref, spread_ref, wide_ref, *tabs):
    step = pl.program_id(0)

    @pl.when(step == 0)
    def _():
        for tab in tabs:
            tab[...] = jnp.zeros_like(tab)
        source = lax.broadcasted_iota(jnp.int32, (CAMS, WIDTH), 0) * 9
        lane = lax.broadcasted_iota(jnp.int32, (CAMS, WIDTH), 1)
        spread = jnp.where((lane >= source) & (lane < source + 9), 1.0, 0.0).astype(jnp.bfloat16)
        spread_ref[0:CAMS, :] = spread
        spread_ref[CAMS : 2 * CAMS, :] = spread

    @pl.when(step < steps)
    def _():
        accumulate(idx_ref, in_ref, pay_ref, tabs)

    @pl.when(step >= steps)
    def _():
        base = pl.multiple_of((step - steps) * FINAL * CAMS, FINAL * CAMS)
        parts = []
        for c in range(FINAL):
            rows = pl.ds(base + c * CAMS, CAMS)
            total = start_ref[rows, :]
            for tab in tabs:
                total = total + tab[rows, :]
            total = total.T[0:FEATS]
            high = total.astype(jnp.bfloat16)
            low = (total - high.astype(jnp.float32)).astype(jnp.bfloat16)
            parts.append(jnp.concatenate([high, low], axis=1))
        wide_ref[...] = jnp.dot(jnp.concatenate(parts, axis=0), spread_ref[...], preferred_element_type=jnp.float32)
        lane = lax.broadcasted_iota(jnp.int32, (8, WIDTH), 1)
        which = lane % 9
        sub = lax.broadcasted_iota(jnp.int32, (8, WIDTH), 0)
        for c in range(FINAL):
            at = c * FEATS
            eight = wide_ref[at : at + 8, :]
            for j in range(1, 9):
                eight = jnp.where(which == j, wide_ref[at + 8 * j : at + 8 * j + 8, :], eight)
            last = jnp.sum(jnp.where(which == sub, wide_ref[at + 72 : at + 80, :], 0.0), axis=0, keepdims=True)
            last = jnp.where(which[0:1] == 8, wide_ref[at + 80 : at + 81, :], last)
            out_ref[0, 9 * c : 9 * c + 8, :] = eight
            out_ref[0, 9 * c + 8 : 9 * c + 9, :] = last


def params(**more):
    return pltpu.CompilerParams(vmem_limit_bytes=VMEM_LIMIT, **more)


def index_of(arrived):
    cell = arrived[:, 36, :] * CAMS + arrived[:, 37, :]
    return cell.astype(jnp.int32).reshape(SIDES // GROUP, 1, GROUP * PTS)


def schur(in0, in1):
    steps = SIDES // GROUP
    cells = CAMS * CAMS
    part = 4096
    spec_idx = pl.BlockSpec((1, 1, GROUP * PTS), lambda s: (jnp.minimum(s, steps - 1), 0, 0), memory_space=pltpu.SMEM)
    spec_in = pl.BlockSpec((GROUP, BLK, PTS), lambda s: (jnp.minimum(s, steps - 1), 0, 0))
    tabs = [pltpu.VMEM((cells, PTS), jnp.float32)] * TABLES
    pay = pltpu.VMEM((GROUP * PTS, PTS), jnp.float32)
    cost = pl.CostEstimate(flops=6 * 10**9, bytes_accessed=12 * 10**6, transcendentals=0)
    total = pl.pallas_call(
        functools.partial(first_kernel, steps),
        grid=(steps + cells // part,),
        in_specs=[spec_idx, spec_in],
        out_specs=pl.BlockSpec((part, PTS), lambda s: (jnp.maximum(s - steps, 0), 0)),
        out_shape=jax.ShapeDtypeStruct((cells, PTS), jnp.float32),
        scratch_shapes=[pay] + tabs,
        compiler_params=params(),
        cost_estimate=cost,
        name="first",
    )(index_of(in0), in0)
    return pl.pallas_call(
        functools.partial(last_kernel, steps),
        grid=(steps + CAMS // FINAL,),
        in_specs=[spec_idx, spec_in, pl.BlockSpec(memory_space=pltpu.VMEM)],
        out_specs=pl.BlockSpec((1, 9 * FINAL, WIDTH), lambda s: (0, jnp.maximum(s - steps, 0), 0)),
        out_shape=jax.ShapeDtypeStruct((1, WIDTH, WIDTH), jnp.float32),
        scratch_shapes=[
            pay,
            pltpu.VMEM((2 * CAMS, WIDTH), jnp.bfloat16),
            pltpu.VMEM((FINAL * FEATS, WIDTH), jnp.float32),
        ]
        + tabs,
        compiler_params=params(),
        cost_estimate=cost,
        name="last",
    )(index_of(in1), in1, total)


def local(cam_jac, pt_jac, resid, damping, cams, block_pair, pair_sides, cluster_home):
    smem = pl.BlockSpec(memory_space=pltpu.SMEM)
    vmem = pl.BlockSpec(memory_space=pltpu.VMEM)
    blocks = cam_jac.shape[0]
    rows, cols = lax.axis_size("row"), lax.axis_size("col")
    tables = (block_pair.reshape(-1), pair_sides.T, cluster_home)
    cam_rows, pt_rows = jnp.transpose(cam_jac, (1, 0, 2)), jnp.transpose(pt_jac, (1, 0, 2))

    def pack(which, *shares):
        return pl.pallas_call(
            functools.partial(pack_kernel, which),
            in_specs=[smem] * 3 + [vmem] * (4 + len(shares)),
            out_specs=vmem,
            out_shape=jax.ShapeDtypeStruct((SIDES, BLK, PTS), jnp.float32),
            scratch_shapes=[
                pltpu.VMEM((blocks * BLK, PTS), jnp.float32),
                pltpu.VMEM((blocks * 8, PTS), jnp.float32),
                pltpu.SMEM((pair_sides.shape[0],), jnp.int32),
            ],
            compiler_params=params(),
            cost_estimate=pl.CostEstimate(flops=10**7, bytes_accessed=6 * 10**6, transcendentals=0),
            name="pack" + str(which),
        )(*tables, cam_rows, pt_rows, damping, cams, *shares)

    in0 = lax.all_to_all(pack(0), RC, 0, 0, tiled=True)

    partial = pl.pallas_call(
        rhs_kernel,
        in_specs=[smem] * 3 + [vmem] * 5,
        out_specs=vmem,
        out_shape=jax.ShapeDtypeStruct((CLUSTERS, 16, CAMS), jnp.float32),
        scratch_shapes=[pltpu.VMEM((blocks * 32, PTS), jnp.float32)],
        compiler_params=params(),
        cost_estimate=pl.CostEstimate(flops=10**10, bytes_accessed=3 * 10**6, transcendentals=0),
        name="rhs",
    )(*tables, cam_rows, pt_rows, resid, damping, cams)
    halves = partial.reshape(rows, CLUSTERS // rows, 16, CAMS)
    core = lax.axis_index("col") % 2
    mine = lax.dynamic_index_in_dim(halves, core, 1, keepdims=False)
    other = lax.dynamic_index_in_dim(halves, 1 - core, 1, keepdims=False)
    mine = mine + lax.ppermute(other, "col", [(c, c ^ 1) for c in range(cols)])
    shares = jnp.transpose(mine.reshape(rows, 16, cols, CAMS // cols), (0, 2, 1, 3))
    in1 = lax.all_to_all(pack(1, shares.reshape(SIDES, 2, PTS)), RC, 0, 0, tiled=True)
    share = jnp.sum(in1[:, 38:40, :].reshape(SIDES // 2, 2, 2, PTS), axis=0).reshape(2, 16, CAMS // cols)
    reduced_rhs = jnp.transpose(share[:, 0:9], (0, 2, 1)).reshape(2, WIDTH // cols)

    return schur(in0, in1), reduced_rhs


def solution(mesh):
    return jax.shard_map(
        local,
        mesh=mesh,
        in_specs=(
            P(RC, None, None),
            P(RC, None, None),
            P(RC, None, None),
            P(RC, None),
            P(RC, None, None),
            P(RC, None),
            P(),
            P(),
        ),
        out_specs=(P(RC, None, None), P("row", "col")),
        check_vma=False,
    )
```

```python
import functools

import jax
import jax.numpy as jnp
from jax import lax
from jax.experimental import pallas as pl
from jax.experimental.pallas import tpu as pltpu
from jax.sharding import PartitionSpec as P

CAMS = 128
PTS = 128
WIDTH = 9 * CAMS
NBR = 4
SIDES = 128
CLUSTERS = 32
BLK = 40
GROUP = 16
TABLES = 6
FINAL = 16
FEATS = 88
VMEM_LIMIT = 62 * 2**20
RC = ("row", "col")


def inverse_of(pt_ref, damp_ref):
    jp = [[[pt_ref[6 * o + 3 * r + k] for k in range(3)] for r in range(2)] for o in range(2)]
    damp = damp_ref[...]

    def entry(a, b):
        total = jp[0][0][a] * jp[0][0][b]
        for o, r in ((0, 1), (1, 0), (1, 1)):
            total = total + jp[o][r][a] * jp[o][r][b]
        return total + damp if a == b else total

    v00, v01, v02, v11, v12, v22 = (entry(a, b) for a, b in ((0, 0), (0, 1), (0, 2), (1, 1), (1, 2), (2, 2)))
    a00 = v11 * v22 - v12 * v12
    a01 = v02 * v12 - v01 * v22
    a02 = v01 * v12 - v02 * v11
    a11 = v00 * v22 - v02 * v02
    a12 = v01 * v02 - v00 * v12
    a22 = v00 * v11 - v01 * v01
    det = v00 * a00 + v01 * a01 + v02 * a02
    inv = [[a00 / det, a01 / det, a02 / det], [a01 / det, a11 / det, a12 / det], [a02 / det, a12 / det, a22 / det]]
    return jp, inv


def slot_of(side, home_ref):
    return home_ref[side // NBR] * NBR + side % NBR


def pack_kernel(which, *refs):
    bp_ref, ps_ref, home_ref, cam_ref, pt_ref, damp_ref, cams_ref = refs[:7]
    share_ref = refs[7] if which else None
    out_ref, rows_ref, turned_ref, seen_ref = refs[-4:]
    blocks = damp_ref.shape[0]
    out_ref[:, 0:36, :] = jnp.zeros((SIDES, 36, PTS), jnp.float32)
    spots = lax.broadcasted_iota(jnp.int32, (SIDES, 4, PTS), 2)
    spots = jnp.where(lax.broadcasted_iota(jnp.int32, (SIDES, 4, PTS), 1) < 2, spots, 0)
    out_ref[:, 36:40, :] = spots.astype(jnp.float32)
    if which:
        out_ref[:, 38:40, :] = share_ref[...]
    jp, inv = inverse_of(pt_ref, damp_ref)
    mix = []
    for r in range(2):
        left = [sum(jp[0][r][k] * inv[k][m] for k in range(3)) for m in range(3)]
        mix.append([-sum(left[m] * jp[1][q][m] for m in range(3)) for q in range(2)])

    def put(row, value):
        rows_ref[pl.ds(row, blocks, stride=BLK), :] = value

    def turn(row, value):
        turned_ref[pl.ds(row, blocks, stride=8), :] = value

    for i in range(9):
        row0, row1 = cam_ref[i], cam_ref[9 + i]
        for q in range(2):
            mixed = row0 * mix[0][q] + row1 * mix[1][q]
            other = cam_ref[18 + 9 * q + i]
            if i < 8:
                put(8 * q + i, mixed)
                put(16 + 8 * q + i, other)
            else:
                put(32 + q, mixed)
                put(34 + q, other)
                turn(2 + q, mixed)
                turn(q, other)
    zero = jnp.zeros((blocks, PTS), jnp.float32)
    for o in range(2):
        ids = cams_ref[:, o, :].astype(jnp.float32)
        put(36 + o, ids)
        turn(5 - o, ids)
        put(38 + o, zero)
        turn(6 + o, zero)
    tops = 38 if which else BLK

    def clear(i, carry):
        seen_ref[i] = 0
        return carry

    lax.fori_loop(0, seen_ref.shape[0], clear, 0)

    def one(t, carry):
        pair = bp_ref[t]
        rank = seen_ref[pair]
        seen_ref[pair] = rank + 1

        @pl.when(rank == which)
        def _():
            first, second = slot_of(ps_ref[0, pair], home_ref), slot_of(ps_ref[1, pair], home_ref)
            base = pl.multiple_of(t * BLK, 8)
            out_ref[first, 0:tops, :] = rows_ref[pl.ds(base, tops), :]
            out_ref[second, 0:16, :] = rows_ref[pl.ds(base + 16, 16), :]
            out_ref[second, 16:32, :] = rows_ref[pl.ds(base, 16), :]
            out_ref[second, 32:tops, :] = turned_ref[pl.ds(pl.multiple_of(t * 8, 8), tops - 32), :]

        return carry

    lax.fori_loop(0, blocks, one, 0)


def rhs_kernel(bp_ref, ps_ref, home_ref, cam_ref, pt_ref, res_ref, damp_ref, cams_ref, out_ref, b_ref):
    blocks = damp_ref.shape[0]
    out_ref[...] = jnp.zeros_like(out_ref)
    b_ref[...] = jnp.zeros_like(b_ref)
    jp, inv = inverse_of(pt_ref, damp_ref)
    err = [[res_ref[:, 2 * o + r, :] for r in range(2)] for o in range(2)]
    gp = [sum(jp[o][r][k] * err[o][r] for o in range(2) for r in range(2)) for k in range(3)]
    z = [sum(inv[k][m] * gp[m] for m in range(3)) for k in range(3)]
    for o in range(2):
        w = [err[o][r] - sum(jp[o][r][k] * z[k] for k in range(3)) for r in range(2)]
        for i in range(9):
            value = cam_ref[18 * o + i] * w[0] + cam_ref[18 * o + 9 + i] * w[1]
            b_ref[pl.ds(16 * o + i, blocks, stride=32), :] = value
    number = lax.broadcasted_iota(jnp.int32, (CAMS, PTS), 0)

    def one(t, carry):
        pair = bp_ref[t]
        for o in range(2):
            home = home_ref[ps_ref[o, pair] // NBR]
            b = b_ref[pl.ds(pl.multiple_of(t * 32, 32) + 16 * o, 16), :]
            high = b.astype(jnp.bfloat16)
            low = (b - high.astype(jnp.float32)).astype(jnp.bfloat16)
            hit = jnp.where(number == cams_ref[t, o : o + 1, :], 1.0, 0.0).astype(jnp.bfloat16)
            added = lax.dot_general(
                jnp.concatenate([high, low], axis=0), hit, (((1,), (1,)), ((), ())), preferred_element_type=jnp.float32
            )
            out_ref[home] = out_ref[home] + (added[0:16] + added[16:32])
        return carry

    lax.fori_loop(0, blocks, one, 0, unroll=4)


def expand(block):
    a0, a1, b0, b1 = block[0:8], block[8:16], block[16:24], block[24:32]
    a08, a18, b08, b18 = block[32:33], block[33:34], block[34:35], block[35:36]
    rows = [a0 * b0[j : j + 1] + a1 * b1[j : j + 1] for j in range(8)]
    rows.append(a0 * b08 + a1 * b18)
    rows.append(a08 * b0 + a18 * b1)
    rows.append(jnp.broadcast_to(a08 * b08 + a18 * b18, (8, PTS)))
    return rows


def fetch(idx_hbm, ids, sem, step, half):
    return pltpu.make_async_copy(idx_hbm.at[2 * step + half], ids[half], sem.at[half])


def accumulate(step, steps, idx_hbm, in_ref, pay_ref, ids, sem, tabs):
    def widen(g):
        rows = expand(in_ref[g])
        rows.append(jnp.zeros((CAMS - FEATS, PTS), jnp.float32))
        pay_ref[g * PTS : (g + 1) * PTS, :] = jnp.concatenate(rows, axis=0).T

    later = jnp.minimum(step + 1, steps - 1)
    widen(0)
    for g in range(GROUP):
        half, place = divmod(g, GROUP // 2)
        if place == 0:
            fetch(idx_hbm, ids, sem, step, half).wait()
        if g + 1 < GROUP:
            widen(g + 1)
        for u in range(PTS):
            i = ids[half][0, place * PTS + u]
            tab = tabs[(g * PTS + u) % TABLES]
            tab[pl.ds(i, 1), :] = tab[pl.ds(i, 1), :] + pay_ref[g * PTS + u : g * PTS + u + 1, :]
        if place == GROUP // 2 - 1:
            fetch(idx_hbm, ids, sem, later, half).start()


def finish_fetch(steps, idx_hbm, ids, sem):
    for half in range(2):
        fetch(idx_hbm, ids, sem, steps - 1, half).wait()


def first_kernel(steps, idx_hbm, in_ref, out_ref, pay_ref, ids0, ids1, sem, *tabs):
    step = pl.program_id(0)
    part = out_ref.shape[0]
    ids = (ids0, ids1)

    @pl.when(step == 0)
    def _():
        for half in range(2):
            fetch(idx_hbm, ids, sem, 0, half).start()
        for tab in tabs:
            tab[...] = jnp.zeros_like(tab)

    @pl.when(step < steps)
    def _():
        accumulate(step, steps, idx_hbm, in_ref, pay_ref, ids, sem, tabs)

    @pl.when(step == steps)
    def _():
        finish_fetch(steps, idx_hbm, ids, sem)

    @pl.when(step >= steps)
    def _():
        rows = pl.ds(pl.multiple_of((step - steps) * part, part), part)
        total = tabs[0][rows, :]
        for tab in tabs[1:]:
            total = total + tab[rows, :]
        out_ref[...] = total


def last_kernel(steps, idx_hbm, in_ref, start_hbm, out_ref, pay_ref, ids0, ids1, sem, spread_ref, wide_ref, got, *tabs):
    step = pl.program_id(0)
    ids = (ids0, ids1)

    @pl.when(step == 0)
    def _():
        for half in range(2):
            fetch(idx_hbm, ids, sem, 0, half).start()
        pltpu.make_async_copy(start_hbm, tabs[0], got).start()
        for tab in tabs[1:]:
            tab[...] = jnp.zeros_like(tab)
        source = lax.broadcasted_iota(jnp.int32, (CAMS, WIDTH), 0) * 9
        lane = lax.broadcasted_iota(jnp.int32, (CAMS, WIDTH), 1)
        spread = jnp.where((lane >= source) & (lane < source + 9), 1.0, 0.0).astype(jnp.bfloat16)
        spread_ref[0:CAMS, :] = spread
        spread_ref[CAMS : 2 * CAMS, :] = spread
        pltpu.make_async_copy(start_hbm, tabs[0], got).wait()

    @pl.when(step < steps)
    def _():
        accumulate(step, steps, idx_hbm, in_ref, pay_ref, ids, sem, tabs)

    @pl.when(step == steps)
    def _():
        finish_fetch(steps, idx_hbm, ids, sem)

    @pl.when(step >= steps)
    def _():
        base = pl.multiple_of((step - steps) * FINAL * CAMS, FINAL * CAMS)
        parts = []
        for c in range(FINAL):
            rows = pl.ds(base + c * CAMS, CAMS)
            total = tabs[0][rows, :]
            for tab in tabs[1:]:
                total = total + tab[rows, :]
            total = total.T[0:FEATS]
            high = total.astype(jnp.bfloat16)
            low = (total - high.astype(jnp.float32)).astype(jnp.bfloat16)
            parts.append(jnp.concatenate([high, low], axis=1))
        wide_ref[...] = jnp.dot(jnp.concatenate(parts, axis=0), spread_ref[...], preferred_element_type=jnp.float32)
        lane = lax.broadcasted_iota(jnp.int32, (8, WIDTH), 1)
        which = lane % 9
        sub = lax.broadcasted_iota(jnp.int32, (8, WIDTH), 0)
        for c in range(FINAL):
            at = c * FEATS
            eight = wide_ref[at : at + 8, :]
            for j in range(1, 9):
                eight = jnp.where(which == j, wide_ref[at + 8 * j : at + 8 * j + 8, :], eight)
            last = jnp.sum(jnp.where(which == sub, wide_ref[at + 72 : at + 80, :], 0.0), axis=0, keepdims=True)
            last = jnp.where(which[0:1] == 8, wide_ref[at + 80 : at + 81, :], last)
            out_ref[0, 9 * c : 9 * c + 8, :] = eight
            out_ref[0, 9 * c + 8 : 9 * c + 9, :] = last


def params(**more):
    return pltpu.CompilerParams(vmem_limit_bytes=VMEM_LIMIT, **more)


def index_of(arrived):
    cell = arrived[:, 36, :] * CAMS + arrived[:, 37, :]
    return cell.astype(jnp.int32).reshape(2 * SIDES // GROUP, 1, GROUP // 2 * PTS)


def schur(in0, in1):
    steps = SIDES // GROUP
    cells = CAMS * CAMS
    part = 4096
    spec_in = pl.BlockSpec((GROUP, BLK, PTS), lambda s: (jnp.minimum(s, steps - 1), 0, 0))
    tabs = [pltpu.VMEM((cells, PTS), jnp.float32)] * TABLES
    own = [
        pltpu.VMEM((GROUP * PTS, PTS), jnp.float32),
        pltpu.SMEM((1, GROUP // 2 * PTS), jnp.int32),
        pltpu.SMEM((1, GROUP // 2 * PTS), jnp.int32),
        pltpu.SemaphoreType.DMA((2,)),
    ]
    hbm = pl.BlockSpec(memory_space=pl.ANY)
    cost = pl.CostEstimate(flops=6 * 10**9, bytes_accessed=12 * 10**6, transcendentals=0)
    total = pl.pallas_call(
        functools.partial(first_kernel, steps),
        grid=(steps + cells // part,),
        in_specs=[hbm, spec_in],
        out_specs=pl.BlockSpec((part, PTS), lambda s: (jnp.maximum(s - steps, 0), 0)),
        out_shape=jax.ShapeDtypeStruct((cells, PTS), jnp.float32),
        scratch_shapes=own + tabs,
        compiler_params=params(),
        cost_estimate=cost,
        name="first",
    )(index_of(in0), in0)
    return pl.pallas_call(
        functools.partial(last_kernel, steps),
        grid=(steps + CAMS // FINAL,),
        in_specs=[hbm, spec_in, hbm],
        out_specs=pl.BlockSpec((1, 9 * FINAL, WIDTH), lambda s: (0, jnp.maximum(s - steps, 0), 0)),
        out_shape=jax.ShapeDtypeStruct((1, WIDTH, WIDTH), jnp.float32),
        scratch_shapes=own
        + [
            pltpu.VMEM((2 * CAMS, WIDTH), jnp.bfloat16),
            pltpu.VMEM((FINAL * FEATS, WIDTH), jnp.float32),
            pltpu.SemaphoreType.DMA(()),
        ]
        + tabs,
        compiler_params=params(),
        cost_estimate=cost,
        name="last",
    )(index_of(in1), in1, total)


def local(cam_jac, pt_jac, resid, damping, cams, block_pair, pair_sides, cluster_home):
    smem = pl.BlockSpec(memory_space=pltpu.SMEM)
    vmem = pl.BlockSpec(memory_space=pltpu.VMEM)
    blocks = cam_jac.shape[0]
    rows, cols = lax.axis_size("row"), lax.axis_size("col")
    tables = (block_pair.reshape(-1), pair_sides.T, cluster_home)
    cam_rows, pt_rows = jnp.transpose(cam_jac, (1, 0, 2)), jnp.transpose(pt_jac, (1, 0, 2))

    def pack(which, *shares):
        return pl.pallas_call(
            functools.partial(pack_kernel, which),
            in_specs=[smem] * 3 + [vmem] * (4 + len(shares)),
            out_specs=vmem,
            out_shape=jax.ShapeDtypeStruct((SIDES, BLK, PTS), jnp.float32),
            scratch_shapes=[
                pltpu.VMEM((blocks * BLK, PTS), jnp.float32),
                pltpu.VMEM((blocks * 8, PTS), jnp.float32),
                pltpu.SMEM((pair_sides.shape[0],), jnp.int32),
            ],
            compiler_params=params(),
            cost_estimate=pl.CostEstimate(flops=10**7, bytes_accessed=6 * 10**6, transcendentals=0),
            name="pack" + str(which),
        )(*tables, cam_rows, pt_rows, damping, cams, *shares)

    in0 = lax.all_to_all(pack(0), RC, 0, 0, tiled=True)

    partial = pl.pallas_call(
        rhs_kernel,
        in_specs=[smem] * 3 + [vmem] * 5,
        out_specs=vmem,
        out_shape=jax.ShapeDtypeStruct((CLUSTERS, 16, CAMS), jnp.float32),
        scratch_shapes=[pltpu.VMEM((blocks * 32, PTS), jnp.float32)],
        compiler_params=params(),
        cost_estimate=pl.CostEstimate(flops=10**10, bytes_accessed=3 * 10**6, transcendentals=0),
        name="rhs",
    )(*tables, cam_rows, pt_rows, resid, damping, cams)
    halves = partial.reshape(rows, CLUSTERS // rows, 16, CAMS)
    core = lax.axis_index("col") % 2
    mine = lax.dynamic_index_in_dim(halves, core, 1, keepdims=False)
    other = lax.dynamic_index_in_dim(halves, 1 - core, 1, keepdims=False)
    mine = mine + lax.ppermute(other, "col", [(c, c ^ 1) for c in range(cols)])
    shares = jnp.transpose(mine.reshape(rows, 16, cols, CAMS // cols), (0, 2, 1, 3))
    in1 = lax.all_to_all(pack(1, shares.reshape(SIDES, 2, PTS)), RC, 0, 0, tiled=True)
    share = jnp.sum(in1[:, 38:40, :].reshape(SIDES // 2, 2, 2, PTS), axis=0).reshape(2, 16, CAMS // cols)
    reduced_rhs = jnp.transpose(share[:, 0:9], (0, 2, 1)).reshape(2, WIDTH // cols)

    return schur(in0, in1), reduced_rhs


def solution(mesh):
    return jax.shard_map(
        local,
        mesh=mesh,
        in_specs=(
            P(RC, None, None),
            P(RC, None, None),
            P(RC, None, None),
            P(RC, None),
            P(RC, None, None),
            P(RC, None),
            P(),
            P(),
        ),
        out_specs=(P(RC, None, None), P("row", "col")),
        check_vma=False,
    )
```

```python
import functools

import jax
import jax.numpy as jnp
from jax import lax
from jax.experimental import pallas as pl
from jax.experimental.pallas import tpu as pltpu
from jax.sharding import PartitionSpec as P

CAMS = 128
PTS = 128
WIDTH = 9 * CAMS
NBR = 4
SIDES = 128
CLUSTERS = 32
BLK = 40
GROUP = 32
TABLES = 2
RUN = 8
FLAG = 1 << 16
FINAL = 32
FEATS = 88
VMEM_LIMIT = 62 * 2**20
RC = ("row", "col")


def inverse_of(pt_ref, damp_ref):
    jp = [[[pt_ref[6 * o + 3 * r + k] for k in range(3)] for r in range(2)] for o in range(2)]
    damp = damp_ref[...]

    def entry(a, b):
        total = jp[0][0][a] * jp[0][0][b]
        for o, r in ((0, 1), (1, 0), (1, 1)):
            total = total + jp[o][r][a] * jp[o][r][b]
        return total + damp if a == b else total

    v00, v01, v02, v11, v12, v22 = (entry(a, b) for a, b in ((0, 0), (0, 1), (0, 2), (1, 1), (1, 2), (2, 2)))
    a00 = v11 * v22 - v12 * v12
    a01 = v02 * v12 - v01 * v22
    a02 = v01 * v12 - v02 * v11
    a11 = v00 * v22 - v02 * v02
    a12 = v01 * v02 - v00 * v12
    a22 = v00 * v11 - v01 * v01
    det = v00 * a00 + v01 * a01 + v02 * a02
    inv = [[a00 / det, a01 / det, a02 / det], [a01 / det, a11 / det, a12 / det], [a02 / det, a12 / det, a22 / det]]
    return jp, inv


def slot_of(side, home_ref):
    return home_ref[side // NBR] * NBR + side % NBR


def pack_kernel(which, *refs):
    bp_ref, ps_ref, home_ref, cam_ref, pt_ref, damp_ref, cams_ref = refs[:7]
    share_ref = refs[7] if which else None
    out_ref, rows_ref, turned_ref, seen_ref = refs[-4:]
    blocks = damp_ref.shape[0]
    out_ref[:, 0:36, :] = jnp.zeros((SIDES, 36, PTS), jnp.float32)
    spots = lax.broadcasted_iota(jnp.int32, (SIDES, 4, PTS), 2)
    spots = jnp.where(lax.broadcasted_iota(jnp.int32, (SIDES, 4, PTS), 1) < 2, spots, 0)
    out_ref[:, 36:40, :] = spots.astype(jnp.float32)
    if which:
        out_ref[:, 38:40, :] = share_ref[...]
    jp, inv = inverse_of(pt_ref, damp_ref)
    mix = []
    for r in range(2):
        left = [sum(jp[0][r][k] * inv[k][m] for k in range(3)) for m in range(3)]
        mix.append([-sum(left[m] * jp[1][q][m] for m in range(3)) for q in range(2)])

    def put(row, value):
        rows_ref[pl.ds(row, blocks, stride=BLK), :] = value

    def turn(row, value):
        turned_ref[pl.ds(row, blocks, stride=8), :] = value

    for i in range(9):
        row0, row1 = cam_ref[i], cam_ref[9 + i]
        for q in range(2):
            mixed = row0 * mix[0][q] + row1 * mix[1][q]
            other = cam_ref[18 + 9 * q + i]
            if i < 8:
                put(8 * q + i, mixed)
                put(16 + 8 * q + i, other)
            else:
                put(32 + q, mixed)
                put(34 + q, other)
                turn(2 + q, mixed)
                turn(q, other)
    zero = jnp.zeros((blocks, PTS), jnp.float32)
    for o in range(2):
        ids = cams_ref[:, o, :].astype(jnp.float32)
        put(36 + o, ids)
        turn(5 - o, ids)
        put(38 + o, zero)
        turn(6 + o, zero)
    tops = 38 if which else BLK

    def write(t):
        pair = bp_ref[t]
        first, second = slot_of(ps_ref[0, pair], home_ref), slot_of(ps_ref[1, pair], home_ref)
        base = pl.multiple_of(t * BLK, 8)
        out_ref[first, 0:tops, :] = rows_ref[pl.ds(base, tops), :]
        out_ref[second, 0:16, :] = rows_ref[pl.ds(base + 16, 16), :]
        out_ref[second, 16:32, :] = rows_ref[pl.ds(base, 16), :]
        out_ref[second, 32:tops, :] = turned_ref[pl.ds(pl.multiple_of(t * 8, 8), tops - 32), :]

    if which == 0:

        def back(n, carry):
            write(blocks - 1 - n)
            return carry

        lax.fori_loop(0, blocks, back, 0, unroll=4)
        return

    def clear(i, carry):
        seen_ref[i] = 0
        return carry

    lax.fori_loop(0, seen_ref.shape[0], clear, 0)

    def one(t, carry):
        pair = bp_ref[t]
        rank = seen_ref[pair]
        seen_ref[pair] = rank + 1
        pl.when(rank == which)(lambda: write(t))
        return carry

    lax.fori_loop(0, blocks, one, 0)


def rhs_kernel(bp_ref, ps_ref, home_ref, cam_ref, pt_ref, res_ref, damp_ref, cams_ref, out_ref, b_ref):
    blocks = damp_ref.shape[0]
    out_ref[...] = jnp.zeros_like(out_ref)
    b_ref[...] = jnp.zeros_like(b_ref)
    jp, inv = inverse_of(pt_ref, damp_ref)
    err = [[res_ref[:, 2 * o + r, :] for r in range(2)] for o in range(2)]
    gp = [sum(jp[o][r][k] * err[o][r] for o in range(2) for r in range(2)) for k in range(3)]
    z = [sum(inv[k][m] * gp[m] for m in range(3)) for k in range(3)]
    for o in range(2):
        w = [err[o][r] - sum(jp[o][r][k] * z[k] for k in range(3)) for r in range(2)]
        for i in range(9):
            value = cam_ref[18 * o + i] * w[0] + cam_ref[18 * o + 9 + i] * w[1]
            b_ref[pl.ds(16 * o + i, blocks, stride=32), :] = value
    number = lax.broadcasted_iota(jnp.int32, (CAMS, PTS), 0)

    def one(t, carry):
        pair = bp_ref[t]
        for o in range(2):
            home = home_ref[ps_ref[o, pair] // NBR]
            b = b_ref[pl.ds(pl.multiple_of(t * 32, 32) + 16 * o, 16), :]
            high = b.astype(jnp.bfloat16)
            low = (b - high.astype(jnp.float32)).astype(jnp.bfloat16)
            hit = jnp.where(number == cams_ref[t, o : o + 1, :], 1.0, 0.0).astype(jnp.bfloat16)
            added = lax.dot_general(
                jnp.concatenate([high, low], axis=0), hit, (((1,), (1,)), ((), ())), preferred_element_type=jnp.float32
            )
            out_ref[home] = out_ref[home] + (added[0:16] + added[16:32])
        return carry

    lax.fori_loop(0, blocks, one, 0, unroll=4)


def expand(block):
    a0, a1, b0, b1 = block[0:8], block[8:16], block[16:24], block[24:32]
    a08, a18, b08, b18 = block[32:33], block[33:34], block[34:35], block[35:36]
    rows = [a0 * b0[j : j + 1] + a1 * b1[j : j + 1] for j in range(8)]
    rows.append(a0 * b08 + a1 * b18)
    rows.append(a08 * b0 + a18 * b1)
    rows.append(jnp.broadcast_to(a08 * b08 + a18 * b18, (8, PTS)))
    return rows


def fetch(cells_ref, ids, sem, step, half):
    rows = pl.ds(pl.multiple_of((2 * step + half) * (GROUP // 2), GROUP // 2), GROUP // 2)
    return pltpu.make_async_copy(cells_ref.at[rows, :], ids[half], sem.at[half])


def name_cells(tail_ref, cells_ref):
    cell = tail_ref[:, 4, :] * CAMS + tail_ref[:, 5, :]
    lane = lax.broadcasted_iota(jnp.int32, (SIDES, PTS), 1)
    hits = jnp.zeros((SIDES, PTS), jnp.float32)
    for r in range(1, RUN):
        same = (cell == pltpu.roll(cell, r, 1)) & (lane % RUN >= r)
        hits = jnp.where(same, 1.0, hits)
    flag = jnp.max(hits, axis=1, keepdims=True) * float(FLAG)
    cells_ref[...] = jnp.where(lane == 0, cell + flag, cell).astype(jnp.int32)


def accumulate(step, steps, in_ref, pay_ref, cells_ref, ids, sem, tabs):
    def widen(g):
        rows = expand(in_ref[g])
        rows.append(jnp.zeros((CAMS - FEATS, PTS), jnp.float32))
        pay_ref[g * PTS : (g + 1) * PTS, :] = jnp.concatenate(rows, axis=0).T

    later = jnp.minimum(step + 1, steps - 1)
    widen(0)
    for g in range(GROUP):
        half, place = divmod(g, GROUP // 2)
        mine = ids[half]
        if place == 0:
            fetch(cells_ref, ids, sem, step, half).wait()
        start = mine[place, 0]

        @pl.when(start < FLAG)
        def _():
            if g + 1 < GROUP:
                widen(g + 1)
            for k in range(PTS // RUN):
                tab = tabs[k % TABLES]
                here = range(k * RUN, (k + 1) * RUN)
                at = [mine[place, u] for u in here]
                old = [tab[pl.ds(i, 1), :] for i in at]
                for u, i, value in zip(here, at, old):
                    tab[pl.ds(i, 1), :] = value + pay_ref[g * PTS + u : g * PTS + u + 1, :]

        @pl.when(start >= FLAG)
        def _():
            if g + 1 < GROUP:
                widen(g + 1)

            def single(u, carry):
                i = mine[place, u]
                i = jnp.where(i >= FLAG, i - FLAG, i)
                tabs[0][pl.ds(i, 1), :] = tabs[0][pl.ds(i, 1), :] + pay_ref[pl.ds(g * PTS + u, 1), :]
                return carry

            lax.fori_loop(0, PTS, single, 0, unroll=8)

        if place == GROUP // 2 - 1:
            fetch(cells_ref, ids, sem, later, half).start()


def finish_fetch(steps, cells_ref, ids, sem):
    for half in range(2):
        fetch(cells_ref, ids, sem, steps - 1, half).wait()


def begin(in_hbm, tail_ref, cells_ref, ids, sem, tail_sem, tabs):
    tail = pltpu.make_async_copy(in_hbm.at[:, 32:40, :], tail_ref, tail_sem)
    tail.start()
    for tab in tabs:
        tab[...] = jnp.zeros_like(tab)
    tail.wait()
    name_cells(tail_ref, cells_ref)
    for half in range(2):
        fetch(cells_ref, ids, sem, 0, half).start()


def first_kernel(steps, in_hbm, in_ref, out_ref, pay_ref, tail_ref, cells_ref, ids0, ids1, sem, tail_sem, *tabs):
    step = pl.program_id(0)
    part = out_ref.shape[0]
    ids = (ids0, ids1)

    @pl.when(step == 0)
    def _():
        begin(in_hbm, tail_ref, cells_ref, ids, sem, tail_sem, tabs)

    @pl.when(step < steps)
    def _():
        accumulate(step, steps, in_ref, pay_ref, cells_ref, ids, sem, tabs)

    @pl.when(step == steps)
    def _():
        finish_fetch(steps, cells_ref, ids, sem)

    @pl.when(step >= steps)
    def _():
        rows = pl.ds(pl.multiple_of((step - steps) * part, part), part)
        total = tabs[0][rows, :]
        for tab in tabs[1:]:
            total = total + tab[rows, :]
        out_ref[...] = total


def collect_rhs(tail_ref, rhs_ref):
    share = rhs_ref.shape[1]
    sums = jnp.sum(tail_ref[...].reshape(SIDES // 2, 2, 8, PTS), axis=0).reshape(16, PTS)
    lane = lax.broadcasted_iota(jnp.int32, (PTS, share), 0)
    place = lax.broadcasted_iota(jnp.int32, (PTS, share), 1)
    eight = jnp.where(place == 9 * (lane % 16) + lane // 16, 1.0, 0.0)
    last = jnp.where((place == 9 * lane + 8) & (lane < 16), 1.0, 0.0)
    exact = lax.Precision.HIGHEST
    upper = jnp.dot(sums, eight, precision=exact, preferred_element_type=jnp.float32)
    lower = jnp.dot(sums, last, precision=exact, preferred_element_type=jnp.float32)
    rhs_ref[0:1, :] = upper[6:7] + lower[7:8]
    rhs_ref[1:2, :] = upper[14:15] + lower[15:16]


def last_kernel(steps, in_hbm, in_ref, start_hbm, out_ref, rhs_ref, pay_ref, tail_ref, cells_ref, ids0, ids1, sem, tail_sem, *refs):
    spread_ref, wide_ref, start_ref, got = refs[:4]
    tabs = refs[4:]
    step = pl.program_id(0)
    ids = (ids0, ids1)

    @pl.when(step == 0)
    def _():
        pltpu.make_async_copy(start_hbm, start_ref, got).start()
        begin(in_hbm, tail_ref, cells_ref, ids, sem, tail_sem, tabs)
        collect_rhs(tail_ref, rhs_ref)
        source = lax.broadcasted_iota(jnp.int32, (CAMS, WIDTH), 0) * 9
        lane = lax.broadcasted_iota(jnp.int32, (CAMS, WIDTH), 1)
        spread = jnp.where((lane >= source) & (lane < source + 9), 1.0, 0.0).astype(jnp.bfloat16)
        spread_ref[0:CAMS, :] = spread
        spread_ref[CAMS : 2 * CAMS, :] = spread

    @pl.when(step < steps)
    def _():
        accumulate(step, steps, in_ref, pay_ref, cells_ref, ids, sem, tabs)

    @pl.when(step == steps)
    def _():
        finish_fetch(steps, cells_ref, ids, sem)
        pltpu.make_async_copy(start_hbm, start_ref, got).wait()

    @pl.when(step >= steps)
    def _():
        base = pl.multiple_of((step - steps) * FINAL * CAMS, FINAL * CAMS)
        parts = []
        for c in range(FINAL):
            rows = pl.ds(base + c * CAMS, CAMS)
            total = start_ref[rows, :]
            for tab in tabs:
                total = total + tab[rows, :]
            total = total.T[0:FEATS]
            high = total.astype(jnp.bfloat16)
            low = (total - high.astype(jnp.float32)).astype(jnp.bfloat16)
            parts.append(jnp.concatenate([high, low], axis=1))
        wide_ref[...] = jnp.dot(jnp.concatenate(parts, axis=0), spread_ref[...], preferred_element_type=jnp.float32)
        lane = lax.broadcasted_iota(jnp.int32, (8, WIDTH), 1)
        which = lane % 9
        sub = lax.broadcasted_iota(jnp.int32, (8, WIDTH), 0)
        for c in range(FINAL):
            at = c * FEATS
            eight = wide_ref[at : at + 8, :]
            for j in range(1, 9):
                eight = jnp.where(which == j, wide_ref[at + 8 * j : at + 8 * j + 8, :], eight)
            last = jnp.sum(jnp.where(which == sub, wide_ref[at + 72 : at + 80, :], 0.0), axis=0, keepdims=True)
            last = jnp.where(which[0:1] == 8, wide_ref[at + 80 : at + 81, :], last)
            out_ref[0, 9 * c : 9 * c + 8, :] = eight
            out_ref[0, 9 * c + 8 : 9 * c + 9, :] = last


def params(**more):
    return pltpu.CompilerParams(vmem_limit_bytes=VMEM_LIMIT, **more)


def schur(in0, in1):
    steps = SIDES // GROUP
    cells = CAMS * CAMS
    part = 8192
    spec_in = pl.BlockSpec((GROUP, BLK, PTS), lambda s: (jnp.minimum(s, steps - 1), 0, 0))
    tabs = [pltpu.VMEM((cells, PTS), jnp.float32)] * TABLES
    half = pltpu.SMEM((GROUP // 2, PTS), jnp.int32)
    own = [
        pltpu.VMEM((GROUP * PTS, PTS), jnp.float32),
        pltpu.VMEM((SIDES, 8, PTS), jnp.float32),
        pltpu.VMEM((SIDES, PTS), jnp.int32),
        half,
        half,
        pltpu.SemaphoreType.DMA((2,)),
        pltpu.SemaphoreType.DMA(()),
    ]
    hbm = pl.BlockSpec(memory_space=pl.ANY)
    cost = pl.CostEstimate(flops=6 * 10**9, bytes_accessed=12 * 10**6, transcendentals=0)
    total = pl.pallas_call(
        functools.partial(first_kernel, steps),
        grid=(steps + cells // part,),
        in_specs=[hbm, spec_in],
        out_specs=pl.BlockSpec((part, PTS), lambda s: (jnp.maximum(s - steps, 0), 0)),
        out_shape=jax.ShapeDtypeStruct((cells, PTS), jnp.float32),
        scratch_shapes=own + tabs,
        compiler_params=params(),
        cost_estimate=cost,
        name="first",
    )(in0, in0)
    return pl.pallas_call(
        functools.partial(last_kernel, steps),
        grid=(steps + CAMS // FINAL,),
        in_specs=[hbm, spec_in, hbm],
        out_specs=[
            pl.BlockSpec((1, 9 * FINAL, WIDTH), lambda s: (0, jnp.maximum(s - steps, 0), 0)),
            pl.BlockSpec((2, WIDTH // 8), lambda s: (0, 0)),
        ],
        out_shape=[
            jax.ShapeDtypeStruct((1, WIDTH, WIDTH), jnp.float32),
            jax.ShapeDtypeStruct((2, WIDTH // 8), jnp.float32),
        ],
        scratch_shapes=own
        + [
            pltpu.VMEM((2 * CAMS, WIDTH), jnp.bfloat16),
            pltpu.VMEM((FINAL * FEATS, WIDTH), jnp.float32),
            pltpu.VMEM((cells, PTS), jnp.float32),
            pltpu.SemaphoreType.DMA(()),
        ]
        + tabs,
        compiler_params=params(),
        cost_estimate=cost,
        name="last",
    )(in1, in1, total)


def local(cam_jac, pt_jac, resid, damping, cams, block_pair, pair_sides, cluster_home):
    smem = pl.BlockSpec(memory_space=pltpu.SMEM)
    vmem = pl.BlockSpec(memory_space=pltpu.VMEM)
    blocks = cam_jac.shape[0]
    rows, cols = lax.axis_size("row"), lax.axis_size("col")
    tables = (block_pair.reshape(-1), pair_sides.T, cluster_home)
    cam_rows, pt_rows = jnp.transpose(cam_jac, (1, 0, 2)), jnp.transpose(pt_jac, (1, 0, 2))

    def pack(which, *shares):
        return pl.pallas_call(
            functools.partial(pack_kernel, which),
            in_specs=[smem] * 3 + [vmem] * (4 + len(shares)),
            out_specs=vmem,
            out_shape=jax.ShapeDtypeStruct((SIDES, BLK, PTS), jnp.float32),
            scratch_shapes=[
                pltpu.VMEM((blocks * BLK, PTS), jnp.float32),
                pltpu.VMEM((blocks * 8, PTS), jnp.float32),
                pltpu.SMEM((pair_sides.shape[0],), jnp.int32),
            ],
            compiler_params=params(),
            cost_estimate=pl.CostEstimate(flops=10**7, bytes_accessed=6 * 10**6, transcendentals=0),
            name="pack" + str(which),
        )(*tables, cam_rows, pt_rows, damping, cams, *shares)

    in0 = lax.all_to_all(pack(0), RC, 0, 0, tiled=True)

    partial = pl.pallas_call(
        rhs_kernel,
        in_specs=[smem] * 3 + [vmem] * 5,
        out_specs=vmem,
        out_shape=jax.ShapeDtypeStruct((CLUSTERS, 16, CAMS), jnp.float32),
        scratch_shapes=[pltpu.VMEM((blocks * 32, PTS), jnp.float32)],
        compiler_params=params(),
        cost_estimate=pl.CostEstimate(flops=10**10, bytes_accessed=3 * 10**6, transcendentals=0),
        name="rhs",
    )(*tables, cam_rows, pt_rows, resid, damping, cams)
    halves = partial.reshape(rows, CLUSTERS // rows, 16, CAMS)
    core = lax.axis_index("col") % 2
    mine = lax.dynamic_index_in_dim(halves, core, 1, keepdims=False)
    other = lax.dynamic_index_in_dim(halves, 1 - core, 1, keepdims=False)
    mine = mine + lax.ppermute(other, "col", [(c, c ^ 1) for c in range(cols)])
    shares = jnp.transpose(mine.reshape(rows, 16, cols, CAMS // cols), (0, 2, 1, 3))
    in1 = lax.all_to_all(pack(1, shares.reshape(SIDES, 2, PTS)), RC, 0, 0, tiled=True)
    return schur(in0, in1)


def solution(mesh):
    return jax.shard_map(
        local,
        mesh=mesh,
        in_specs=(
            P(RC, None, None),
            P(RC, None, None),
            P(RC, None, None),
            P(RC, None),
            P(RC, None, None),
            P(RC, None),
            P(),
            P(),
        ),
        out_specs=(P(RC, None, None), P("row", "col")),
        check_vma=False,
    )
```

```python
import functools

import jax
import jax.numpy as jnp
from jax import lax
from jax.experimental import pallas as pl
from jax.experimental.pallas import tpu as pltpu
from jax.sharding import PartitionSpec as P

CAMS = 128
PTS = 128
WIDTH = 9 * CAMS
NBR = 4
SIDES = 128
CLUSTERS = 32
BLK = 40
GROUP = 32
TABLES = 2
RUN = 8
FLAG = 1 << 16
FINAL = 32
PART = 16
FEATS = 88
VMEM_LIMIT = 62 * 2**20
RC = ("row", "col")


def inverse_of(pt_ref, damp_ref):
    jp = [[[pt_ref[6 * o + 3 * r + k] for k in range(3)] for r in range(2)] for o in range(2)]
    damp = damp_ref[...]

    def entry(a, b):
        total = jp[0][0][a] * jp[0][0][b]
        for o, r in ((0, 1), (1, 0), (1, 1)):
            total = total + jp[o][r][a] * jp[o][r][b]
        return total + damp if a == b else total

    v00, v01, v02, v11, v12, v22 = (entry(a, b) for a, b in ((0, 0), (0, 1), (0, 2), (1, 1), (1, 2), (2, 2)))
    a00 = v11 * v22 - v12 * v12
    a01 = v02 * v12 - v01 * v22
    a02 = v01 * v12 - v02 * v11
    a11 = v00 * v22 - v02 * v02
    a12 = v01 * v02 - v00 * v12
    a22 = v00 * v11 - v01 * v01
    det = v00 * a00 + v01 * a01 + v02 * a02
    inv = [[a00 / det, a01 / det, a02 / det], [a01 / det, a11 / det, a12 / det], [a02 / det, a12 / det, a22 / det]]
    return jp, inv


def slot_of(side, home_ref):
    return home_ref[side // NBR] * NBR + side % NBR


def pack_kernel(which, *refs):
    bp_ref, ps_ref, home_ref, cam_ref, pt_ref, damp_ref, cams_ref = refs[:7]
    share_ref = refs[7] if which else None
    out_ref, rows_ref, turned_ref, seen_ref = refs[-4:]
    blocks = damp_ref.shape[0]
    out_ref[:, 0:36, :] = jnp.zeros((SIDES, 36, PTS), jnp.float32)
    spots = lax.broadcasted_iota(jnp.int32, (SIDES, 4, PTS), 2)
    spots = jnp.where(lax.broadcasted_iota(jnp.int32, (SIDES, 4, PTS), 1) < 2, spots, 0)
    out_ref[:, 36:40, :] = spots.astype(jnp.float32)
    if which:
        out_ref[:, 38:40, :] = share_ref[...]
    jp, inv = inverse_of(pt_ref, damp_ref)
    mix = []
    for r in range(2):
        left = [sum(jp[0][r][k] * inv[k][m] for k in range(3)) for m in range(3)]
        mix.append([-sum(left[m] * jp[1][q][m] for m in range(3)) for q in range(2)])

    def put(row, value):
        rows_ref[pl.ds(row, blocks, stride=BLK), :] = value

    def turn(row, value):
        turned_ref[pl.ds(row, blocks, stride=8), :] = value

    for i in range(9):
        row0, row1 = cam_ref[i], cam_ref[9 + i]
        for q in range(2):
            mixed = row0 * mix[0][q] + row1 * mix[1][q]
            other = cam_ref[18 + 9 * q + i]
            if i < 8:
                put(8 * q + i, mixed)
                put(16 + 8 * q + i, other)
            else:
                put(32 + q, mixed)
                put(34 + q, other)
                turn(2 + q, mixed)
                turn(q, other)
    zero = jnp.zeros((blocks, PTS), jnp.float32)
    for o in range(2):
        ids = cams_ref[:, o, :].astype(jnp.float32)
        put(36 + o, ids)
        turn(5 - o, ids)
        put(38 + o, zero)
        turn(6 + o, zero)
    tops = 38 if which else BLK

    def write(t):
        pair = bp_ref[t]
        first, second = slot_of(ps_ref[0, pair], home_ref), slot_of(ps_ref[1, pair], home_ref)
        base = pl.multiple_of(t * BLK, 8)
        out_ref[first, 0:tops, :] = rows_ref[pl.ds(base, tops), :]
        out_ref[second, 0:16, :] = rows_ref[pl.ds(base + 16, 16), :]
        out_ref[second, 16:32, :] = rows_ref[pl.ds(base, 16), :]
        out_ref[second, 32:tops, :] = turned_ref[pl.ds(pl.multiple_of(t * 8, 8), tops - 32), :]

    if which == 0:

        def back(n, carry):
            write(blocks - 1 - n)
            return carry

        lax.fori_loop(0, blocks, back, 0, unroll=4)
        return

    def clear(i, carry):
        seen_ref[i] = 0
        return carry

    lax.fori_loop(0, seen_ref.shape[0], clear, 0)

    def one(t, carry):
        pair = bp_ref[t]
        rank = seen_ref[pair]
        seen_ref[pair] = rank + 1
        pl.when(rank == which)(lambda: write(t))
        return carry

    lax.fori_loop(0, blocks, one, 0)


def rhs_kernel(bp_ref, ps_ref, home_ref, cam_ref, pt_ref, res_ref, damp_ref, cams_ref, out_ref, b_ref):
    blocks = damp_ref.shape[0]
    out_ref[...] = jnp.zeros_like(out_ref)
    b_ref[...] = jnp.zeros_like(b_ref)
    jp, inv = inverse_of(pt_ref, damp_ref)
    err = [[res_ref[:, 2 * o + r, :] for r in range(2)] for o in range(2)]
    gp = [sum(jp[o][r][k] * err[o][r] for o in range(2) for r in range(2)) for k in range(3)]
    z = [sum(inv[k][m] * gp[m] for m in range(3)) for k in range(3)]
    for o in range(2):
        w = [err[o][r] - sum(jp[o][r][k] * z[k] for k in range(3)) for r in range(2)]
        for i in range(9):
            value = cam_ref[18 * o + i] * w[0] + cam_ref[18 * o + 9 + i] * w[1]
            b_ref[pl.ds(16 * o + i, blocks, stride=32), :] = value
    number = lax.broadcasted_iota(jnp.int32, (CAMS, PTS), 0)

    def one(t, carry):
        pair = bp_ref[t]
        for o in range(2):
            home = home_ref[ps_ref[o, pair] // NBR]
            b = b_ref[pl.ds(pl.multiple_of(t * 32, 32) + 16 * o, 16), :]
            high = b.astype(jnp.bfloat16)
            low = (b - high.astype(jnp.float32)).astype(jnp.bfloat16)
            hit = jnp.where(number == cams_ref[t, o : o + 1, :], 1.0, 0.0).astype(jnp.bfloat16)
            added = lax.dot_general(
                jnp.concatenate([high, low], axis=0), hit, (((1,), (1,)), ((), ())), preferred_element_type=jnp.float32
            )
            out_ref[home] = out_ref[home] + (added[0:16] + added[16:32])
        return carry

    lax.fori_loop(0, blocks, one, 0, unroll=4)


def expand(block):
    a0, a1, b0, b1 = block[0:8], block[8:16], block[16:24], block[24:32]
    a08, a18, b08, b18 = block[32:33], block[33:34], block[34:35], block[35:36]
    rows = [a0 * b0[j : j + 1] + a1 * b1[j : j + 1] for j in range(8)]
    rows.append(a0 * b08 + a1 * b18)
    rows.append(a08 * b0 + a18 * b1)
    rows.append(jnp.broadcast_to(a08 * b08 + a18 * b18, (8, PTS)))
    return rows


def fetch(cells_ref, ids, sem, step, half):
    rows = pl.ds(pl.multiple_of((2 * step + half) * (GROUP // 2), GROUP // 2), GROUP // 2)
    return pltpu.make_async_copy(cells_ref.at[rows, :], ids[half], sem.at[half])


def name_cells(tail_ref, cells_ref):
    cell = tail_ref[:, 4, :] * CAMS + tail_ref[:, 5, :]
    lane = lax.broadcasted_iota(jnp.int32, (SIDES, PTS), 1)
    hits = jnp.zeros((SIDES, PTS), jnp.float32)
    for r in range(1, RUN):
        same = (cell == pltpu.roll(cell, r, 1)) & (lane % RUN >= r)
        hits = jnp.where(same, 1.0, hits)
    flag = jnp.max(hits, axis=1, keepdims=True) * float(FLAG)
    cells_ref[...] = jnp.where(lane == 0, cell + flag, cell).astype(jnp.int32)


def accumulate(step, steps, in_ref, pay_ref, cells_ref, ids, sem, tabs):
    def widen(g):
        rows = expand(in_ref[g])
        rows.append(jnp.zeros((CAMS - FEATS, PTS), jnp.float32))
        pay_ref[g * PTS : (g + 1) * PTS, :] = jnp.concatenate(rows, axis=0).T

    later = jnp.minimum(step + 1, steps - 1)
    widen(0)
    for g in range(GROUP):
        half, place = divmod(g, GROUP // 2)
        mine = ids[half]
        if place == 0:
            fetch(cells_ref, ids, sem, step, half).wait()
        start = mine[place, 0]

        @pl.when(start < FLAG)
        def _():
            if g + 1 < GROUP:
                widen(g + 1)
            for k in range(PTS // RUN):
                tab = tabs[k % TABLES]
                here = range(k * RUN, (k + 1) * RUN)
                at = [mine[place, u] for u in here]
                old = [tab[pl.ds(i, 1), :] for i in at]
                for u, i, value in zip(here, at, old):
                    tab[pl.ds(i, 1), :] = value + pay_ref[g * PTS + u : g * PTS + u + 1, :]

        @pl.when(start >= FLAG)
        def _():
            if g + 1 < GROUP:
                widen(g + 1)

            def several(n, carry):
                for v in range(8):
                    u = n * 8 + v
                    tab = tabs[v % TABLES]
                    i = mine[place, u]
                    i = jnp.where(i >= FLAG, i - FLAG, i)
                    tab[pl.ds(i, 1), :] = tab[pl.ds(i, 1), :] + pay_ref[pl.ds(g * PTS + u, 1), :]
                return carry

            lax.fori_loop(0, PTS // 8, several, 0)

        if place == GROUP // 2 - 1:
            fetch(cells_ref, ids, sem, later, half).start()


def finish_fetch(steps, cells_ref, ids, sem):
    for half in range(2):
        fetch(cells_ref, ids, sem, steps - 1, half).wait()


def begin(in_hbm, tail_ref, cells_ref, ids, sem, tail_sem, tabs):
    tail = pltpu.make_async_copy(in_hbm.at[:, 32:40, :], tail_ref, tail_sem)
    tail.start()
    for tab in tabs:
        tab[...] = jnp.zeros_like(tab)
    tail.wait()
    name_cells(tail_ref, cells_ref)
    for half in range(2):
        fetch(cells_ref, ids, sem, 0, half).start()


def first_kernel(steps, in_hbm, in_ref, out_ref, pay_ref, tail_ref, cells_ref, ids0, ids1, sem, tail_sem, *tabs):
    step = pl.program_id(0)
    part = out_ref.shape[0]
    ids = (ids0, ids1)

    @pl.when(step == 0)
    def _():
        begin(in_hbm, tail_ref, cells_ref, ids, sem, tail_sem, tabs)

    @pl.when(step < steps)
    def _():
        accumulate(step, steps, in_ref, pay_ref, cells_ref, ids, sem, tabs)

    @pl.when(step == steps)
    def _():
        finish_fetch(steps, cells_ref, ids, sem)

    @pl.when(step >= steps)
    def _():
        rows = pl.ds(pl.multiple_of((step - steps) * part, part), part)
        total = tabs[0][rows, :]
        for tab in tabs[1:]:
            total = total + tab[rows, :]
        out_ref[...] = total


def collect_rhs(tail_ref, rhs_ref):
    share = rhs_ref.shape[1]
    sums = jnp.sum(tail_ref[...].reshape(SIDES // 2, 2, 8, PTS), axis=0).reshape(16, PTS)
    lane = lax.broadcasted_iota(jnp.int32, (PTS, share), 0)
    place = lax.broadcasted_iota(jnp.int32, (PTS, share), 1)
    eight = jnp.where(place == 9 * (lane % 16) + lane // 16, 1.0, 0.0)
    last = jnp.where((place == 9 * lane + 8) & (lane < 16), 1.0, 0.0)
    exact = lax.Precision.HIGHEST
    upper = jnp.dot(sums, eight, precision=exact, preferred_element_type=jnp.float32)
    lower = jnp.dot(sums, last, precision=exact, preferred_element_type=jnp.float32)
    rhs_ref[0:1, :] = upper[6:7] + lower[7:8]
    rhs_ref[1:2, :] = upper[14:15] + lower[15:16]


def last_kernel(steps, in_hbm, in_ref, start_hbm, out_ref, rhs_ref, pay_ref, tail_ref, cells_ref, ids0, ids1, sem, tail_sem, *refs):
    spread_ref, wide_ref, start_ref, got = refs[:4]
    tabs = refs[4:]
    step = pl.program_id(0)
    ids = (ids0, ids1)

    @pl.when(step == 0)
    def _():
        pltpu.make_async_copy(start_hbm, start_ref, got).start()
        begin(in_hbm, tail_ref, cells_ref, ids, sem, tail_sem, tabs)
        collect_rhs(tail_ref, rhs_ref)
        source = lax.broadcasted_iota(jnp.int32, (CAMS, WIDTH), 0) * 9
        lane = lax.broadcasted_iota(jnp.int32, (CAMS, WIDTH), 1)
        spread = jnp.where((lane >= source) & (lane < source + 9), 1.0, 0.0).astype(jnp.bfloat16)
        spread_ref[0:CAMS, :] = spread
        spread_ref[CAMS : 2 * CAMS, :] = spread

    @pl.when(step < steps)
    def _():
        accumulate(step, steps, in_ref, pay_ref, cells_ref, ids, sem, tabs)

    @pl.when(step == steps)
    def _():
        finish_fetch(steps, cells_ref, ids, sem)
        pltpu.make_async_copy(start_hbm, start_ref, got).wait()

    @pl.when(step >= steps)
    def _():
        base = pl.multiple_of((step - steps) * FINAL * CAMS, FINAL * CAMS)
        lane = lax.broadcasted_iota(jnp.int32, (8, WIDTH), 1)
        which = lane % 9
        sub = lax.broadcasted_iota(jnp.int32, (8, WIDTH), 0)

        def turned(part):
            pieces = []
            for c in range(part * PART, (part + 1) * PART):
                rows = pl.ds(base + c * CAMS, CAMS)
                total = start_ref[rows, :]
                for tab in tabs:
                    total = total + tab[rows, :]
                total = total.T[0:FEATS]
                high = total.astype(jnp.bfloat16)
                low = (total - high.astype(jnp.float32)).astype(jnp.bfloat16)
                pieces.append(jnp.concatenate([high, low], axis=1))
            return jnp.concatenate(pieces, axis=0)

        def spread_out(part, left):
            rows = slice(part * PART * FEATS, (part + 1) * PART * FEATS)
            wide_ref[rows, :] = jnp.dot(left, spread_ref[...], preferred_element_type=jnp.float32)

        def pick(part):
            for c in range(part * PART, (part + 1) * PART):
                at = c * FEATS
                eight = wide_ref[at : at + 8, :]
                for j in range(1, 9):
                    eight = jnp.where(which == j, wide_ref[at + 8 * j : at + 8 * j + 8, :], eight)
                last = jnp.sum(jnp.where(which == sub, wide_ref[at + 72 : at + 80, :], 0.0), axis=0, keepdims=True)
                last = jnp.where(which[0:1] == 8, wide_ref[at + 80 : at + 81, :], last)
                out_ref[0, 9 * c : 9 * c + 8, :] = eight
                out_ref[0, 9 * c + 8 : 9 * c + 9, :] = last

        left = turned(0)
        for part in range(FINAL // PART):
            spread_out(part, left)
            if part + 1 < FINAL // PART:
                left = turned(part + 1)
            if part:
                pick(part - 1)
        pick(FINAL // PART - 1)


def params(**more):
    return pltpu.CompilerParams(vmem_limit_bytes=VMEM_LIMIT, **more)


def schur(in0, in1):
    steps = SIDES // GROUP
    cells = CAMS * CAMS
    part = 8192
    spec_in = pl.BlockSpec((GROUP, BLK, PTS), lambda s: (jnp.minimum(s, steps - 1), 0, 0))
    tabs = [pltpu.VMEM((cells, PTS), jnp.float32)] * TABLES
    half = pltpu.SMEM((GROUP // 2, PTS), jnp.int32)
    own = [
        pltpu.VMEM((GROUP * PTS, PTS), jnp.float32),
        pltpu.VMEM((SIDES, 8, PTS), jnp.float32),
        pltpu.VMEM((SIDES, PTS), jnp.int32),
        half,
        half,
        pltpu.SemaphoreType.DMA((2,)),
        pltpu.SemaphoreType.DMA(()),
    ]
    hbm = pl.BlockSpec(memory_space=pl.ANY)
    cost = pl.CostEstimate(flops=6 * 10**9, bytes_accessed=12 * 10**6, transcendentals=0)
    total = pl.pallas_call(
        functools.partial(first_kernel, steps),
        grid=(steps + cells // part,),
        in_specs=[hbm, spec_in],
        out_specs=pl.BlockSpec((part, PTS), lambda s: (jnp.maximum(s - steps, 0), 0)),
        out_shape=jax.ShapeDtypeStruct((cells, PTS), jnp.float32),
        scratch_shapes=own + tabs,
        compiler_params=params(),
        cost_estimate=cost,
        name="first",
    )(in0, in0)
    return pl.pallas_call(
        functools.partial(last_kernel, steps),
        grid=(steps + CAMS // FINAL,),
        in_specs=[hbm, spec_in, hbm],
        out_specs=[
            pl.BlockSpec((1, 9 * FINAL, WIDTH), lambda s: (0, jnp.maximum(s - steps, 0), 0)),
            pl.BlockSpec((2, WIDTH // 8), lambda s: (0, 0)),
        ],
        out_shape=[
            jax.ShapeDtypeStruct((1, WIDTH, WIDTH), jnp.float32),
            jax.ShapeDtypeStruct((2, WIDTH // 8), jnp.float32),
        ],
        scratch_shapes=own
        + [
            pltpu.VMEM((2 * CAMS, WIDTH), jnp.bfloat16),
            pltpu.VMEM((FINAL * FEATS, WIDTH), jnp.float32),
            pltpu.VMEM((cells, PTS), jnp.float32),
            pltpu.SemaphoreType.DMA(()),
        ]
        + tabs,
        compiler_params=params(),
        cost_estimate=cost,
        name="last",
    )(in1, in1, total)


def local(cam_jac, pt_jac, resid, damping, cams, block_pair, pair_sides, cluster_home):
    smem = pl.BlockSpec(memory_space=pltpu.SMEM)
    vmem = pl.BlockSpec(memory_space=pltpu.VMEM)
    blocks = cam_jac.shape[0]
    rows, cols = lax.axis_size("row"), lax.axis_size("col")
    tables = (block_pair.reshape(-1), pair_sides.T, cluster_home)
    cam_rows, pt_rows = jnp.transpose(cam_jac, (1, 0, 2)), jnp.transpose(pt_jac, (1, 0, 2))

    def pack(which, *shares):
        return pl.pallas_call(
            functools.partial(pack_kernel, which),
            in_specs=[smem] * 3 + [vmem] * (4 + len(shares)),
            out_specs=vmem,
            out_shape=jax.ShapeDtypeStruct((SIDES, BLK, PTS), jnp.float32),
            scratch_shapes=[
                pltpu.VMEM((blocks * BLK, PTS), jnp.float32),
                pltpu.VMEM((blocks * 8, PTS), jnp.float32),
                pltpu.SMEM((pair_sides.shape[0],), jnp.int32),
            ],
            compiler_params=params(),
            cost_estimate=pl.CostEstimate(flops=10**7, bytes_accessed=6 * 10**6, transcendentals=0),
            name="pack" + str(which),
        )(*tables, cam_rows, pt_rows, damping, cams, *shares)

    in0 = lax.all_to_all(pack(0), RC, 0, 0, tiled=True)

    partial = pl.pallas_call(
        rhs_kernel,
        in_specs=[smem] * 3 + [vmem] * 5,
        out_specs=vmem,
        out_shape=jax.ShapeDtypeStruct((CLUSTERS, 16, CAMS), jnp.float32),
        scratch_shapes=[pltpu.VMEM((blocks * 32, PTS), jnp.float32)],
        compiler_params=params(),
        cost_estimate=pl.CostEstimate(flops=10**10, bytes_accessed=3 * 10**6, transcendentals=0),
        name="rhs",
    )(*tables, cam_rows, pt_rows, resid, damping, cams)
    halves = partial.reshape(rows, CLUSTERS // rows, 16, CAMS)
    core = lax.axis_index("col") % 2
    mine = lax.dynamic_index_in_dim(halves, core, 1, keepdims=False)
    other = lax.dynamic_index_in_dim(halves, 1 - core, 1, keepdims=False)
    mine = mine + lax.ppermute(other, "col", [(c, c ^ 1) for c in range(cols)])
    shares = jnp.transpose(mine.reshape(rows, 16, cols, CAMS // cols), (0, 2, 1, 3))
    in1 = lax.all_to_all(pack(1, shares.reshape(SIDES, 2, PTS)), RC, 0, 0, tiled=True)
    return schur(in0, in1)


def solution(mesh):
    return jax.shard_map(
        local,
        mesh=mesh,
        in_specs=(
            P(RC, None, None),
            P(RC, None, None),
            P(RC, None, None),
            P(RC, None),
            P(RC, None, None),
            P(RC, None),
            P(),
            P(),
        ),
        out_specs=(P(RC, None, None), P("row", "col")),
        check_vma=False,
    )
```
